32 devices in a mesh: dp: 8 (over y, x, core), mp: 4 (over z).
Axes of the slice: x: 2, y: 2, z: 4, core: 2. Of those that a mesh axis runs over, the one named last changes fastest.
Arguments:
- hidden: bfloat16 [16384, 1024], P('dp'), may hold values from -6 to 6
- lengths: int32 [8, 8], P('dp'), may hold values from 0 to 2048, as said below
- query_weight: bfloat16 [1024, 1024], P(None, 'mp'), may hold values from -0.1875 to 0.1875
- query_bias: float32 [1024], P('mp'), may hold values from -3 to 3
- key_weight: bfloat16 [1024, 1024], P(None, 'mp'), may hold values from -0.1875 to 0.1875
- key_bias: float32 [1024], P('mp'), may hold values from -3 to 3
- value_weight: bfloat16 [1024, 1024], P(None, 'mp'), may hold values from -0.1875 to 0.1875
- value_bias: float32 [1024], P('mp'), may hold values from -3 to 3
- out_weight: bfloat16 [1024, 1024], P('mp'), may hold values from -0.75 to 0.75
- out_bias: float32 [1024], replicated, may hold values from -3 to 3
- first_gain: float32 [1024], replicated, may hold values from 0.5 to 1.5
- first_shift: float32 [1024], replicated, may hold values from -3 to 3
- up_weight: bfloat16 [1024, 4096], P(None, 'mp'), may hold values from -0.1875 to 0.1875
- up_bias: float32 [4096], P('mp'), may hold values from -3 to 3
- down_weight: bfloat16 [4096, 1024], P('mp'), may hold values from -0.09375 to 0.09375
- down_bias: float32 [1024], replicated, may hold values from -3 to 3
- second_gain: float32 [1024], replicated, may hold values from 0.5 to 1.5
- second_shift: float32 [1024], replicated, may hold values from -3 to 3
- out_grad: bfloat16 [16384, 1024], P('dp'), may hold values from -6 to 6
Outputs:
- result: bfloat16 [16384, 1024], P('dp')
- hidden_grad: bfloat16 [16384, 1024], P('dp')
- query_weight_grad: float32 [1024, 1024], P(None, 'mp')
- query_bias_grad: float32 [1024], P('mp')
- key_weight_grad: float32 [1024, 1024], P(None, 'mp')
- key_bias_grad: float32 [1024], P('mp')
- value_weight_grad: float32 [1024, 1024], P(None, 'mp')
- value_bias_grad: float32 [1024], P('mp')
- out_weight_grad: float32 [1024, 1024], P('mp')
- out_bias_grad: float32 [1024], replicated
- first_gain_grad: float32 [1024], replicated
- first_shift_grad: float32 [1024], replicated
- up_weight_grad: float32 [1024, 4096], P(None, 'mp')
- up_bias_grad: float32 [4096], P('mp')
- down_weight_grad: float32 [4096, 1024], P('mp')
- down_bias_grad: float32 [1024], replicated
- second_gain_grad: float32 [1024], replicated
- second_shift_grad: float32 [1024], replicated
The draws below stay inside these ranges and needn't reach their ends.
Inputs may be any that keep to these rules, and one draw needn't show every extreme that they name: Row r lists the lengths of the sequences packed in order from the start of the r-th block of 2048 slots; every length is 0 (an unused slot) or a multiple of 64; a row sums to at most 2048, and the slots after its sum are padding.
All inputs are finite; a program needn't handle non-finite values.
Results may differ from the reference program's by a relative error of at most 0.03.
Values may be sent and summed in bfloat16 or wider, within the bound.
No kernel may reach another device: no remote copies, remote signals or barrier semaphores. Data moves between devices by JAX's collectives and lax.ppermute only.
A program may use at most 192 MiB of HBM per device.

```python
import math
import jax
import jax.numpy as jnp
from jax import lax

D = 1024
HEADS = 16
HEAD = 64
FF = 4096
ROWS = 2048
SEQS = 8
UNIT = 64
TOKENS = 16384
N_DP = 8
N_MP = 4


def draw_lengths(key, part):
    key = jax.random.fold_in(key, 7)
    subkeys = jax.random.split(key, 5)
    units_all = ROWS // UNIT
    baseline = jax.random.randint(subkeys[0], (N_DP,), units_all // 3 + 1, units_all // 2 + 1)
    additional = jax.random.randint(subkeys[1], (N_DP,), 0, units_all // 2 + 1) * jax.random.randint(subkeys[2], (N_DP,), 0, 2)
    unit_count = jnp.minimum(baseline + additional, units_all)
    fullest = jax.random.randint(subkeys[3], (), 0, N_DP)
    is_full = jnp.arange(N_DP, dtype=jnp.int32) == fullest
    unit_count = jnp.where(is_full, units_all, unit_count)
    cut_points = jax.random.randint(subkeys[4], (N_DP, SEQS - 1), 0, units_all + 1)
    cut_points = jnp.sort(jnp.minimum(cut_points, unit_count[:, None]), axis=1)
    boundaries = jnp.concatenate([jnp.zeros((N_DP, 1), jnp.int32), cut_points, unit_count[:, None]], axis=1)
    lengths = (boundaries[:, 1:] - boundaries[:, :-1]) * UNIT
    single_row = jnp.concatenate([jnp.full((N_DP, 1), ROWS, jnp.int32), jnp.zeros((N_DP, SEQS - 1), jnp.int32)], axis=1)
    return jnp.where(is_full[:, None], single_row, lengths).astype(jnp.int32)


def level_of(stream_key, dims, cuts, smallest, top_value):
    loudness, own = 1.0, jax.random.fold_in(stream_key, 6)
    for dim, parts in cuts:
        draws = jnp.exp(jax.random.uniform(jax.random.fold_in(own, dim), (parts,), jnp.float32, smallest / len(cuts), top_value / len(cuts)))
        loudness = loudness * jnp.repeat(draws, dims[dim] // parts).reshape([-1 if axis == dim else 1 for axis in range(len(dims))])
    return loudness


def scatter_about(rng, extent, scale, most, cuts=(), kind=jnp.bfloat16):
    loudness = level_of(rng, extent, cuts, -0.22, 0.18) if cuts else 1.0
    array = jax.random.normal(rng, extent, jnp.float32) * scale * loudness
    return jnp.minimum(jnp.maximum(array, -most), most).astype(kind)


def setup_inputs(seed: int = 0) -> dict:
    keys = jax.random.split(jax.random.key(seed), 20)
    hidden = scatter_about(keys[0], (TOKENS, D), 1.0, 6.0, ((0, 8),))
    lengths = draw_lengths(jax.random.fold_in(keys[19], 71), 0)
    query_weight = scatter_about(keys[2], (D, D), D ** -0.5, 0.1875, ((1, 4),))
    query_bias = scatter_about(keys[3], (D,), 0.5, 3.0, ((0, 4),), jnp.float32)
    key_weight = scatter_about(keys[4], (D, D), D ** -0.5, 0.1875, ((1, 4),))
    key_bias = scatter_about(keys[5], (D,), 0.5, 3.0, ((0, 4),), jnp.float32)
    value_weight = scatter_about(keys[6], (D, D), D ** -0.5, 0.1875, ((1, 4),))
    value_bias = scatter_about(keys[7], (D,), 0.5, 3.0, ((0, 4),), jnp.float32)
    out_weight = scatter_about(keys[8], (D, D), (D // 16) ** -0.5, 0.75, ((0, 4),))
    out_bias = scatter_about(keys[9], (D,), 0.5, 3.0, (), jnp.float32)
    first_gain = jnp.clip(1.0 + 0.1 * jax.random.normal(keys[10], (D,), jnp.float32), 0.5, 1.5)
    first_shift = scatter_about(keys[11], (D,), 0.5, 3.0, (), jnp.float32)
    up_weight = scatter_about(keys[12], (D, FF), D ** -0.5, 0.1875, ((1, 4),))
    up_bias = scatter_about(keys[13], (FF,), 0.5, 3.0, ((0, 4),), jnp.float32)
    down_weight = scatter_about(keys[14], (FF, D), FF ** -0.5, 0.09375, ((0, 4),))
    down_bias = scatter_about(keys[15], (D,), 0.5, 3.0, (), jnp.float32)
    second_gain = jnp.clip(1.0 + 0.1 * jax.random.normal(keys[16], (D,), jnp.float32), 0.5, 1.5)
    second_shift = scatter_about(keys[17], (D,), 0.5, 3.0, (), jnp.float32)
    out_grad = scatter_about(keys[18], (TOKENS, D), 1.0, 6.0, ((0, 8),))
    return dict(hidden=hidden, lengths=lengths, query_weight=query_weight, query_bias=query_bias, key_weight=key_weight, key_bias=key_bias, value_weight=value_weight, value_bias=value_bias, out_weight=out_weight, out_bias=out_bias, first_gain=first_gain, first_shift=first_shift, up_weight=up_weight, up_bias=up_bias, down_weight=down_weight, down_bias=down_bias, second_gain=second_gain, second_shift=second_shift, out_grad=out_grad)


@jax.custom_vjp
def low(v):
    return lax.optimization_barrier(v.astype(jnp.bfloat16)).astype(jnp.float32)

@jax.custom_vjp
def low_back(v):
    return v

def low_keep(v):
    return (low(v), None)

def low_pass(kept, grad):
    return (grad,)

def back_keep(v):
    return (v, None)

def back_low(kept, grad):
    return (low(grad),)
low.defvjp(low_keep, low_pass)
low_back.defvjp(back_keep, back_low)
epsilon = 1e-06
precise = lax.Precision.HIGHEST

def layout(lengths_row, row_count):
    seq_ends = jnp.cumsum(lengths_row)
    token_index = jnp.arange(row_count, dtype=jnp.int32)
    segment = lax.optimization_barrier(jnp.sum((token_index[:, None] >= seq_ends[None, :]).astype(jnp.int32), axis=1))
    is_valid = token_index < seq_ends[-1]
    starts = lax.optimization_barrier(jnp.max(jnp.where(seq_ends[None, :] <= token_index[:, None], seq_ends[None, :], 0), axis=1))
    position = (token_index - starts).astype(jnp.float32)
    return (segment, is_valid, position)

def rotate(matrix, position, head_size, direction):
    row_count = matrix.shape[0]
    half_size = head_size // 2
    frequency = 10000.0 ** (-2.0 * jnp.arange(half_size, dtype=jnp.float32) / head_size)
    angles = position[:, None] * frequency[None, :]
    cosine = jnp.cos(angles)[:, None, :]
    sine_term = direction * jnp.sin(angles)[:, None, :]
    pair_view = matrix.reshape(row_count, -1, half_size, 2)
    former = pair_view[..., 0]
    latter = pair_view[..., 1]
    turned = jnp.stack([former * cosine - latter * sine_term, latter * cosine + former * sine_term], axis=-1)
    return turned.reshape(row_count, -1)

def layer_norm(summed, gain_row, shift_row):
    row_mean = lax.optimization_barrier(jnp.mean(summed, axis=-1, keepdims=True))
    centered = summed - row_mean
    variance = lax.optimization_barrier(jnp.mean(centered * centered, axis=-1, keepdims=True))
    inv_std = lax.rsqrt(variance + epsilon)
    normed = centered * inv_std
    return normed * gain_row + shift_row

def attend_rows(queries, keys_all, values_all, segment, is_valid, start_row, block_rows):
    query_part = lax.dynamic_slice_in_dim(queries, start_row, block_rows, 0)
    segment_part = lax.dynamic_slice_in_dim(segment, start_row, block_rows, 0)
    valid_part = lax.dynamic_slice_in_dim(is_valid, start_row, block_rows, 0)
    score_scale = 1.0 / math.sqrt(HEAD)
    raw_scores = low_back(jnp.einsum('qhd,khd->hqk', query_part, keys_all, precision=precise) * score_scale)
    allowed = (segment_part[:, None] == segment[None, :]) & valid_part[:, None] & is_valid[None, :]
    masked = jnp.where(allowed[None], raw_scores, -1e+30)
    row_top = jnp.where(valid_part[None, :], lax.optimization_barrier(jnp.max(masked, axis=-1)), 0.0)
    weights_exp = jnp.exp(masked - row_top[..., None])
    row_total = lax.optimization_barrier(jnp.sum(weights_exp, axis=-1)) + (1.0 - valid_part.astype(jnp.float32))[None, :]
    attention = weights_exp / row_total[..., None]
    return jnp.einsum('hqk,khd->qhd', low(attention), values_all, precision=precise)

def forward(inputs, params, segment, is_valid, position):
    query_weight, query_bias, key_weight, key_bias, value_weight, value_bias, out_weight, out_bias, first_gain, first_shift, up_weight, up_bias, down_weight, down_bias, second_gain, second_shift = params
    row_count = inputs.shape[0]
    queries = low(rotate(low_back(jnp.dot(inputs, query_weight, precision=precise) + query_bias), position, HEAD, 1.0))
    keys_all = low(rotate(low_back(jnp.dot(inputs, key_weight, precision=precise) + key_bias), position, HEAD, 1.0))
    values_all = low(low_back(jnp.dot(inputs, value_weight, precision=precise) + value_bias))
    queries = queries.reshape(row_count, HEADS, HEAD)
    keys_all = keys_all.reshape(row_count, HEADS, HEAD)
    values_all = values_all.reshape(row_count, HEADS, HEAD)
    block_rows = min(512, row_count)
    starts = jnp.arange(row_count // block_rows, dtype=jnp.int32) * block_rows

    def one_block(start_row):
        return attend_rows(queries, keys_all, values_all, segment, is_valid, start_row, block_rows)
    context = lax.map(jax.checkpoint(one_block), starts).reshape(row_count, D)
    context = low(low_back(context))
    partials = jnp.einsum('rgc,gcd->grd', context.reshape(row_count, N_MP, D // N_MP), out_weight.reshape(N_MP, D // N_MP, D), precision=precise)
    attended = low_back(lax.optimization_barrier(jnp.sum(low(partials), axis=0)) + out_bias)
    first = layer_norm(inputs + attended, first_gain, first_shift)
    upper = low_back(jnp.dot(low(first), up_weight, precision=precise) + up_bias)
    activated = low(jax.nn.gelu(upper, approximate=False))
    partials_down = jnp.einsum('rgc,gcd->grd', activated.reshape(row_count, N_MP, FF // N_MP), down_weight.reshape(N_MP, FF // N_MP, D), precision=precise)
    lowered = low_back(lax.optimization_barrier(jnp.sum(low(partials_down), axis=0)) + down_bias)
    return layer_norm(first + lowered, second_gain, second_shift)

def reference(hidden, lengths, query_weight, query_bias, key_weight, key_bias, value_weight, value_bias, out_weight, out_bias, first_gain, first_shift, up_weight, up_bias, down_weight, down_bias, second_gain, second_shift, out_grad):
    params = tuple((item.astype(jnp.float32) for item in (query_weight, query_bias, key_weight, key_bias, value_weight, value_bias, out_weight, out_bias, first_gain, first_shift, up_weight, up_bias, down_weight, down_bias, second_gain, second_shift)))
    blocks_in = hidden.reshape(N_DP, ROWS, D)
    blocks_grad = out_grad.reshape(N_DP, ROWS, D)

    def block_step(carried, pieces):
        block_in, lengths_row, block_grad = pieces
        segment, is_valid, position = layout(lengths_row, ROWS)

        def run_block(inputs, weights):
            return forward(inputs, weights, segment, is_valid, position)
        output, pullback = jax.vjp(run_block, block_in.astype(jnp.float32), params)
        input_grad, weight_grads = pullback(block_grad.astype(jnp.float32))
        carried = jax.tree.map(lambda running, addend: running + addend, carried, weight_grads)
        return (carried, (output.astype(jnp.bfloat16), input_grad.astype(jnp.bfloat16)))
    zero_grads = jax.tree.map(jnp.zeros_like, params)
    totals, outputs = lax.scan(block_step, zero_grads, (blocks_in, lengths, blocks_grad))
    result = outputs[0].reshape(TOKENS, D)
    hidden_grad = outputs[1].reshape(TOKENS, D)
    return (result, hidden_grad, totals[0], totals[1], totals[2], totals[3], totals[4], totals[5], totals[6], totals[7], totals[8], totals[9], totals[10], totals[11], totals[12], totals[13], totals[14], totals[15])
```

```python
import functools
import math

import jax
import jax.numpy as jnp
from jax import lax
from jax.experimental import pallas as pl
from jax.experimental.pallas import tpu as pltpu
from jax.sharding import PartitionSpec as P

HEAD = 64
HALF = HEAD // 2
LANES = 128
FEAT = 16
FAR = -1e30
FLOOR = -1e29
LOG2E = 1.4426950408889634
LN2 = 0.6931471805599453
VMEM_LIMIT = 60 * 1024 * 1024
epsilon = 1e-06
f32 = jnp.float32
bf16 = jnp.bfloat16


def params(*semantics):
    return pltpu.CompilerParams(
        dimension_semantics=semantics, vmem_limit_bytes=VMEM_LIMIT
    )


def nn(a, b):
    return lax.dot_general(a, b, (((1,), (0,)), ((), ())), preferred_element_type=f32)


def nt(a, b):
    return lax.dot_general(a, b, (((1,), (1,)), ((), ())), preferred_element_type=f32)


def tn(a, b):
    return lax.dot_general(a, b, (((0,), (0,)), ((), ())), preferred_element_type=f32)


def interleave_matrix(transposed):
    row = lax.broadcasted_iota(jnp.int32, (HEAD, HEAD), 0)
    col = lax.broadcasted_iota(jnp.int32, (HEAD, HEAD), 1)
    if transposed:
        row, col = col, row
    source = jnp.where(row < HALF, 2 * row, 2 * (row - HALF) + 1)
    return jnp.where(col == source, 1.0, 0.0).astype(bf16)


def project_kernel(
    heads, lengths_ref, hidden_ref, qw_ref, kw_ref, vw_ref, qb_ref, kb_ref, vb_ref,
    qt_ref, kt_ref, kn_ref, vt_ref, vn_ref, cos_ref, sin_ref, turned_ref, wt_ref, bias_ref,
):
    width = heads * HEAD
    rows = hidden_ref.shape[0]

    @pl.when(pl.program_id(0) == 0)
    def _():
        split = interleave_matrix(False)
        for index, weight in enumerate((qw_ref, kw_ref)):
            for h in range(heads):
                turned = weight[:, h * HEAD:(h + 1) * HEAD]
                wt_ref[index * width + h * HEAD:index * width + (h + 1) * HEAD, :] = nt(
                    split, turned
                ).astype(bf16)
        for index, weight in enumerate((qw_ref, kw_ref, vw_ref)):
            turned = weight[...].astype(f32).T.astype(bf16)
            for h in range(heads):
                at = (3 * h + index) * HEAD
                turned_ref[at:at + HEAD] = turned[h * HEAD:(h + 1) * HEAD]
        wt_ref[2 * width:, :] = turned
        same = jnp.where(
            lax.broadcasted_iota(jnp.int32, (HEAD, HEAD), 0)
            == lax.broadcasted_iota(jnp.int32, (HEAD, HEAD), 1),
            1.0,
            0.0,
        )
        chosen = (split.astype(f32), split.astype(f32), same)
        for index, source in enumerate((qb_ref, kb_ref, vb_ref)):
            for h in range(heads):
                part = source[:, h * HEAD:(h + 1) * HEAD]
                bias_ref[index * width + h * HEAD:index * width + (h + 1) * HEAD, :] = jnp.sum(
                    chosen[index] * part, axis=1, keepdims=True
                )

    token = lax.broadcasted_iota(jnp.int32, (8, rows), 1) + pl.program_id(0) * rows
    end = jnp.int32(0)
    segment = jnp.zeros((8, rows), jnp.int32)
    start = jnp.zeros((8, rows), jnp.int32)
    for j in range(lengths_ref.shape[1]):
        end = end + lengths_ref[0, j]
        past = token >= end
        segment = segment + past.astype(jnp.int32)
        start = jnp.where(past, jnp.maximum(start, end), start)
    valid = (token < end)[:1]
    segment = segment[:1]
    same = lax.broadcasted_iota(jnp.int32, (FEAT, rows), 0) == segment
    query_side = jnp.where(same, 1.0, 0.0).astype(bf16)
    key_side = jnp.where(same & valid, 0.0, FAR)
    position = (token - start)[:1].astype(f32)
    pair = lax.broadcasted_iota(jnp.int32, (HALF, rows), 0).astype(f32)
    angle = jnp.exp(pair * (-2.0 * math.log(10000.0) / HEAD)) * position
    cosine, sine = jnp.cos(angle), jnp.sin(angle)
    cos_ref[...] = cosine
    sin_ref[...] = sine
    lane_row = lax.broadcasted_iota(jnp.int32, (LANES - HEAD - FEAT, rows), 0)
    tail = jnp.where(lane_row < 3, 1.0, 0.0)
    ones_row = lax.broadcasted_iota(jnp.int32, (LANES - HEAD, rows), 0)
    projected = nt(wt_ref[...], hidden_ref[...]) + bias_ref[...]
    for h in range(heads):
        for index in range(2):
            base = index * width + h * HEAD
            former = projected[base:base + HALF]
            latter = projected[base + HALF:base + HEAD]
            turned_a = former * cosine - latter * sine
            turned_b = latter * cosine + former * sine
            if index == 0:
                scale = LOG2E / math.sqrt(HEAD)
                qt_ref[h] = jnp.concatenate(
                    [
                        (turned_a * scale).astype(bf16),
                        (turned_b * scale).astype(bf16),
                        query_side,
                        jnp.zeros((LANES - HEAD - FEAT, rows), bf16),
                    ],
                    axis=0,
                )
            else:
                kt_ref[h] = jnp.concatenate([turned_a, turned_b], axis=0).astype(bf16)
                kn_ref[h] = (
                    jnp.concatenate([turned_a, turned_b, key_side, tail], axis=0)
                    .T.astype(bf16)
                )
        base = 2 * width + h * HEAD
        flat = projected[base:base + HEAD]
        ones = jnp.where((ones_row >= 3 * h) & (ones_row < 3 * h + 3), 1.0, 0.0)
        vt_ref[h] = jnp.concatenate([flat, jnp.ones((FEAT, rows), f32)], axis=0).astype(bf16)
        vn_ref[h] = jnp.concatenate([flat, ones], axis=0).T.astype(bf16)


def project(lengths, hidden, qw, kw, vw, qb, kb, vb):
    rows, depth = hidden.shape
    width = qw.shape[1]
    heads = width // HEAD
    block = min(512, rows)
    whole = lambda *shape: pl.BlockSpec(shape, lambda i: (0,) * len(shape))
    table = pl.BlockSpec((HALF, block), lambda i: (0, i))
    return pl.pallas_call(
        functools.partial(project_kernel, heads),
        grid=(rows // block,),
        in_specs=[pl.BlockSpec(memory_space=pltpu.SMEM)]
        + [pl.BlockSpec((block, depth), lambda i: (i, 0))]
        + [whole(depth, width)] * 3
        + [whole(1, width)] * 3,
        out_specs=[
            pl.BlockSpec((heads, LANES, block), lambda i: (0, 0, i)),
            pl.BlockSpec((heads, HEAD, block), lambda i: (0, 0, i)),
            pl.BlockSpec((heads, block, LANES), lambda i: (0, i, 0)),
            pl.BlockSpec((heads, HEAD + FEAT, block), lambda i: (0, 0, i)),
            pl.BlockSpec((heads, block, LANES), lambda i: (0, i, 0)),
            table,
            table,
            whole(3 * width, depth),
        ],
        out_shape=[
            jax.ShapeDtypeStruct((heads, LANES, rows), bf16),
            jax.ShapeDtypeStruct((heads, HEAD, rows), bf16),
            jax.ShapeDtypeStruct((heads, rows, LANES), bf16),
            jax.ShapeDtypeStruct((heads, HEAD + FEAT, rows), bf16),
            jax.ShapeDtypeStruct((heads, rows, LANES), bf16),
            jax.ShapeDtypeStruct((HALF, rows), f32),
            jax.ShapeDtypeStruct((HALF, rows), f32),
            jax.ShapeDtypeStruct((3 * width, depth), bf16),
        ],
        scratch_shapes=[
            pltpu.VMEM((3 * width, depth), bf16), pltpu.VMEM((3 * width, 1), f32)
        ],
        compiler_params=params("arbitrary"),
        cost_estimate=pl.CostEstimate(
            flops=6 * rows * depth * width, bytes_accessed=16 * rows * depth, transcendentals=0
        ),
        name="project",
    )(lengths, hidden, qw, kw, vw, qb[None], kb[None], vb[None])


def pack_kernel(chips, me_ref, up_ref, down_ref, out_ref, bias_ref, pack_ref, sems):
    depth, local = up_ref.shape
    half, width = local // 2, out_ref.shape[0]
    core, chip = me_ref[1] & 1, me_ref[1] >> 1
    ups, downs, outs = depth // chips, half // chips, width // (2 * chips)
    row = pl.multiple_of(chip * ups, ups)
    pieces = [(up_ref, row, ups, pl.multiple_of(core * half, half))]
    row = pl.multiple_of(core * half + chip * downs, downs)
    pieces += [(down_ref, row, downs, c * half) for c in range(2)]
    row = pl.multiple_of(core * (width // 2) + chip * outs, outs)
    pieces += [(out_ref, row, outs, c * half) for c in range(2)]
    at, copies = 0, []
    for i, (source, row, extent, column) in enumerate(pieces):
        copies.append(
            pltpu.make_async_copy(
                source.at[pl.ds(row, extent), pl.ds(column, half)],
                pack_ref.at[at:at + extent],
                sems.at[i],
            )
        )
        at += extent
    for copy in copies:
        copy.start()
    row = lax.broadcasted_iota(jnp.int32, (FEAT, half), 0)
    total = jnp.zeros((FEAT, half), f32)
    for c in range(2):
        total = total + split_rows(bias_ref[:, c * half:(c + 1) * half], FEAT, half, 3 * c)
    pack_ref[at:] = total.astype(bf16)
    for copy in copies:
        copy.wait()


def make_pack(me, chips, up, down, out, bias):
    depth, local = up.shape
    half, width = local // 2, out.shape[0]
    rows = depth // chips + 2 * (half // chips + width // (2 * chips)) + FEAT
    hbm = pl.BlockSpec(memory_space=pl.ANY)
    vmem = pl.BlockSpec(memory_space=pltpu.VMEM)
    return pl.pallas_call(
        functools.partial(pack_kernel, chips),
        in_specs=[pl.BlockSpec(memory_space=pltpu.SMEM), hbm, hbm, hbm, vmem],
        out_specs=vmem,
        out_shape=jax.ShapeDtypeStruct((rows, half), bf16),
        scratch_shapes=[pltpu.SemaphoreType.DMA((5,))],
        name="pack",
    )(me, up, down, out, bias[None])


def attend_kernel(heads, me_ref, qt_ref, kn_ref, vt_ref, *refs):
    ctx_ref, lse_ref = refs[-2:]
    for h in range(heads):
        scores = nn(kn_ref[h], qt_ref[h])
        top = jnp.maximum(jnp.max(scores, axis=0, keepdims=True), FLOOR)
        weights = jnp.exp2(scores - top).astype(bf16)
        mixed = nn(vt_ref[h], weights)
        total = mixed[HEAD:HEAD + 1] + jnp.where(top <= FLOOR, 1.0, 0.0)
        ctx_ref[0, h * HEAD:(h + 1) * HEAD] = (mixed[:HEAD] / total).astype(bf16)
        lse_ref[0, h] = top + jnp.log2(total)


def attend(me, first, count, n_mp, qt, kn, vt, after):
    heads, _, rows = qt.shape
    own = rows // n_mp
    block = min(256, own)
    blocks = own // block
    whole = lambda *shape: pl.BlockSpec(shape, lambda i, me: (0,) * len(shape))
    return pl.pallas_call(
        functools.partial(attend_kernel, heads),
        grid_spec=pltpu.PrefetchScalarGridSpec(
            num_scalar_prefetch=1,
            grid=(count * blocks,),
            in_specs=[
                pl.BlockSpec(
                    (heads, LANES, block),
                    lambda i, me: (
                        0, 0, (me[0] ^ (first - i // blocks)) * blocks + i % blocks
                    ),
                ),
                whole(heads, rows, LANES),
                whole(heads, HEAD + FEAT, rows),
            ]
            + [pl.BlockSpec(memory_space=pl.ANY)] * len(after),
            out_specs=[
                pl.BlockSpec(
                    (1, heads * HEAD, block), lambda i, me: (i // blocks, 0, i % blocks)
                ),
                pl.BlockSpec(
                    (1, heads, 1, block), lambda i, me: (i // blocks, 0, 0, i % blocks)
                ),
            ],
        ),
        out_shape=[
            jax.ShapeDtypeStruct((count, heads * HEAD, own), bf16),
            jax.ShapeDtypeStruct((count, heads, 1, own), f32),
        ],
        compiler_params=params("arbitrary"),
        cost_estimate=pl.CostEstimate(
            flops=20 * heads * own * rows * HEAD * count,
            bytes_accessed=8 * rows * LANES * heads,
            transcendentals=heads * own * rows * count,
        ),
        name="attend",
    )(me, qt, kn, vt, *after)


def split_rows(value, count, rows, first):
    high = value.astype(bf16).astype(f32)
    rest = value - high
    middle = rest.astype(bf16).astype(f32)
    low = rest - middle
    row = lax.broadcasted_iota(jnp.int32, (count, rows), 0) - first
    return jnp.where(
        row == 0, high, jnp.where(row == 1, middle, jnp.where(row == 2, low, 0.0))
    )


def attend_back_kernel(
    chunk, me_ref, qt_ref, kt_ref, kn_ref, vn_ref, dot_ref, delta_ref, lse_ref, cosq_ref, sinq_ref,
    cos_ref, sin_ref, *refs,
):
    dq_ref, dk_ref, dv_ref, send_ref, dk_acc, dv_acc = refs[-6:]
    outer, inner = pl.program_id(0), pl.program_id(1)
    rows = kn_ref.shape[1]
    block = qt_ref.shape[2]
    query = qt_ref[0, :HEAD]
    grad = dot_ref[0]
    query_full = jnp.concatenate(
        [
            qt_ref[0, :HEAD + FEAT],
            split_rows(-lse_ref[0, 0], FEAT, block, 0).astype(bf16),
            jnp.zeros((LANES - HEAD - 2 * FEAT, block), bf16),
        ],
        axis=0,
    )
    grad_full = jnp.concatenate(
        [grad, delta_ref[0], jnp.zeros((LANES - HEAD - FEAT, block), bf16)], axis=0
    )

    @pl.when((outer == 0) & (inner == 0))
    def _():
        dk_acc[...] = jnp.zeros_like(dk_acc)
        dv_acc[...] = jnp.zeros_like(dv_acc)

    total = None
    for start in range(0, rows, chunk):
        part = slice(start, start + chunk)
        weights = jnp.exp2(nn(kn_ref[0, part], query_full))
        slopes = nn(vn_ref[0, part], grad_full)
        score_grad = (weights * slopes).astype(bf16)
        dv_acc[:, part] += nt(grad, weights.astype(bf16))
        dk_acc[:, part] += nt(query, score_grad)
        piece = nn(kt_ref[0, :, part], score_grad)
        total = piece if total is None else total + piece
    merge = interleave_matrix(True)

    def turn_back(value, cosine, sine, scale):
        former = value[:HALF] * scale
        latter = value[HALF:] * scale
        turned = jnp.concatenate(
            [former * cosine + latter * sine, latter * cosine - former * sine], axis=0
        )
        return nn(merge, turned.astype(bf16)).astype(bf16)

    dq = turn_back(total, cosq_ref[...], sinq_ref[...], 1.0 / math.sqrt(HEAD))
    dq_ref[...] = dq
    send_ref[outer, :HEAD, pl.ds(pl.multiple_of(inner * block, block), block)] = dq

    @pl.when((outer == pl.num_programs(0) - 1) & (inner == pl.num_programs(1) - 1))
    def _():
        dk = turn_back(dk_acc[...], cos_ref[...], sin_ref[...], LN2)
        dv = dv_acc[...].astype(bf16)
        dk_ref[...] = dk
        dv_ref[...] = dv
        count, _, own = send_ref.shape
        for j in range(count):
            send_ref[j, HEAD:2 * HEAD] = dk[:, j * own:(j + 1) * own]
            send_ref[j, 2 * HEAD:] = dv[:, j * own:(j + 1) * own]


def attend_back(me, head, n_mp, qt, kt, kn, vn, grads, lse, cosine, sine, after):
    heads, _, rows = qt.shape
    width = heads * HEAD
    own = rows // n_mp
    block = min(256, own)
    blocks = own // block
    chunk = min(512, rows)
    place = lambda j, i: j * blocks + i
    by_head = lambda *shape: pl.BlockSpec((1,) + shape, lambda j, i, me: (head, 0, 0))
    whole = lambda *shape: pl.BlockSpec(shape, lambda j, i, me: (0,) * len(shape))
    here = lambda count: pl.BlockSpec((count, block), lambda j, i, me: (0, place(j, i)))
    return pl.pallas_call(
        functools.partial(attend_back_kernel, chunk),
        grid_spec=pltpu.PrefetchScalarGridSpec(
            num_scalar_prefetch=1,
            grid=(n_mp, blocks),
            in_specs=[
                pl.BlockSpec((1, LANES, block), lambda j, i, me: (head, 0, place(j, i))),
                by_head(HEAD, rows),
                by_head(rows, LANES),
                by_head(rows, LANES),
                pl.BlockSpec((1, HEAD, block), lambda j, i, me: (j, head, i)),
                pl.BlockSpec((1, FEAT, block), lambda j, i, me: (j, width // FEAT, i)),
                pl.BlockSpec((1, 1, 1, block), lambda j, i, me: (me[0] ^ j, head, 0, i)),
                here(HALF),
                here(HALF),
                whole(HALF, rows),
                whole(HALF, rows),
            ]
            + [pl.BlockSpec(memory_space=pl.ANY)] * len(after),
            out_specs=[
                here(HEAD), whole(HEAD, rows), whole(HEAD, rows), whole(n_mp, 3 * HEAD, own)
            ],
            scratch_shapes=[pltpu.VMEM((HEAD, rows), f32)] * 2,
        ),
        out_shape=[jax.ShapeDtypeStruct((HEAD, rows), bf16)] * 3
        + [jax.ShapeDtypeStruct((n_mp, 3 * HEAD, own), bf16)],
        compiler_params=params("arbitrary", "arbitrary"),
        cost_estimate=pl.CostEstimate(
            flops=80 * rows * rows * HEAD,
            bytes_accessed=8 * rows * LANES,
            transcendentals=rows * rows,
        ),
        name="attend_back",
    )(me, qt, kt, kn, vn, grads, grads, lse, cosine, sine, cosine, sine, *after)


def gelu_parts(value):
    cumulative = 0.5 * (1.0 + lax.erf(value * 0.7071067811865476))
    density = jnp.exp(-0.5 * value * value) * 0.3989422804014327
    return value * cumulative, cumulative + value * density


def row_mean(value):
    return jnp.mean(value, axis=-1, keepdims=True)


def plane_orders(count):
    bits = [1 << b for b in range(count.bit_length() - 1)]
    orders = []
    for sequence in (bits, bits[::-1]):
        held = [0]
        for bit in sequence:
            held = held + [r ^ bit for r in held]
        orders.append(held)
    return orders


def weight_copies(n_mp, packed, splits, me_ref, weights, banks, targets, sems):
    depth, local = weights[1].shape
    width = weights[0].shape[0]
    copies = [[[], [], []] for _ in range(n_mp)]
    for m, source in enumerate(weights):
        copies[0][m].append(
            pltpu.make_async_copy(source, targets[m].at[0], sems.at[0, m, 0])
        )
    for s in range(1, n_mp):
        if not packed:
            for m in range(3):
                copies[s][m].append(
                    pltpu.make_async_copy(
                        banks[m].at[s - 1], targets[m].at[s], sems.at[s, m, 0]
                    )
                )
            continue
        group = max(i for i in range(len(splits) - 1) if splits[i] <= s)
        member = s - splits[group]
        half, chips = local // 2, packed // 2
        ups, downs, outs = depth // chips, half // chips, width // packed
        orders = plane_orders(chips)
        for core in range(2):
            mine = (me_ref[1] & 1) ^ core
            for r in range(chips):
                for kind in range(2):
                    source = banks[4 * group + 2 * core + kind].at[r, member]
                    chip = (me_ref[1] >> 1) ^ orders[kind][r]
                    if kind == 0:
                        pieces = [(1, 0, ups, chip * ups, mine * half)]
                    else:
                        at = pl.multiple_of(mine * half + chip * downs, downs)
                        pieces = [(2, c * downs, downs, at, c * half) for c in range(2)]
                        at = mine * (width // 2) + chip * outs
                        pieces += [
                            (0, 2 * downs + c * outs, outs, at, c * half) for c in range(2)
                        ]
                    for m, start, extent, row, column in pieces:
                        row = pl.multiple_of(row, extent)
                        if m == 1:
                            column = pl.multiple_of(column, half)
                        copies[s][m].append(
                            pltpu.make_async_copy(
                                source.at[start:start + extent],
                                targets[m].at[s, pl.ds(row, extent), pl.ds(column, half)],
                                sems.at[s, m, len(copies[s][m])],
                            )
                        )
    return copies


def column(value):
    return jnp.sum(value, axis=0, keepdims=True)


def run_all(groups, action):
    for group in groups:
        for copy in group:
            getattr(copy, action)()


def feed_kernel(n_mp, packed, splits, me_ref, hidden_ref, cot_ref, *refs):
    refs = list(refs)
    take = lambda count: [refs.pop(0) for _ in range(count)]
    contexts = take(n_mp)
    weights = take(3)
    banks = take(4 * (len(splits) - 1) if packed else 3)
    bias_ref, vectors_ref = take(2)
    (
        result_ref, first_low_ref, act_ref, slope_ref, lg_ref, normed_ref, inv_ref, back_ref,
        vec_ref, out_s, up_s, down_s, first_s, sems,
    ) = refs
    depth, local = weights[1].shape
    own = hidden_ref.shape[0]
    width = weights[0].shape[0]
    step = min(512, local)
    copies = weight_copies(
        n_mp, packed, splits, me_ref, weights, banks, (out_s, up_s, down_s), sems
    )
    for m in range(3):
        run_all([copies[s][m] for s in range(n_mp)], "start")
    run_all([copies[s][0] for s in range(n_mp)], "wait")

    out_bias, first_gain, first_shift, down_bias, second_gain, second_shift = (
        vectors_ref[i:i + 1, :] for i in range(6)
    )
    summed = hidden_ref[...].astype(f32) + out_bias
    for s in range(n_mp):
        summed = summed + tn(contexts[s][:width], out_s[s])
    centered = summed - row_mean(summed)
    first_inv = lax.rsqrt(row_mean(centered * centered) + epsilon)
    inv_ref[...] = jnp.broadcast_to(first_inv, inv_ref.shape)
    normed = centered * first_inv
    normed_ref[...] = normed
    first = normed * first_gain + first_shift
    first_s[...] = first
    first_low_ref[...] = first.astype(bf16)

    lowered = None
    for s in range(n_mp):
        run_all(copies[s][1:], "wait")
        for start in range(0, local, step):
            part = slice(start, start + step)
            upper = nn(first_low_ref[...], up_s[s, :, part]) + bias_ref[s:s + 1, part]
            value, slope = gelu_parts(upper)
            act = value.astype(bf16)
            act_ref[s, :, part] = act
            slope_ref[s, :, part] = slope.astype(bf16)
            piece = nn(act, down_s[s, part, :])
            lowered = piece if lowered is None else lowered + piece

    summed = first_s[...] + (lowered + down_bias)
    centered = summed - row_mean(summed)
    second_inv = lax.rsqrt(row_mean(centered * centered) + epsilon)
    normed = centered * second_inv
    result_ref[...] = (normed * second_gain + second_shift).astype(bf16)
    cotangent = cot_ref[...].astype(f32)
    grad = cotangent * second_gain
    back = second_inv * (grad - row_mean(grad) - normed * row_mean(grad * normed))
    back_ref[...] = back
    low = back.astype(bf16)
    lg_ref[...] = low
    vec_ref[0:1] = column(low.astype(f32))
    vec_ref[1:2] = column(cotangent * normed)
    vec_ref[2:3] = column(cotangent)


def feed_back_kernel(n_mp, packed, splits, me_ref, *refs):
    refs = list(refs)
    take = lambda count: [refs.pop(0) for _ in range(count)]
    contexts = take(n_mp)
    weights = take(3)
    banks = take(4 * (len(splits) - 1) if packed else 3)
    slope_ref, lg_ref, normed_ref, inv_ref, second_ref, some_ref, gain_ref = take(7)
    ug_ref, ag_ref, back_ref, dctx_ref, vec_ref, out_s, up_s, down_s, sems = refs[-9:]
    depth, local = weights[1].shape
    own = lg_ref.shape[0]
    width = weights[0].shape[0]
    heads = width // HEAD
    step = min(512, local)
    copies = weight_copies(
        n_mp, packed, splits, me_ref, weights, banks, (out_s, up_s, down_s), sems
    )
    for s in range(n_mp):
        run_all(copies[s][:0:-1], "start")
    run_all([copies[s][0] for s in range(n_mp)], "start")

    first_grad = second_ref[...]
    up_bias_grads = []
    for s in range(n_mp):
        run_all(copies[s][:0:-1], "wait")
        sums = []
        for start in range(0, local, step):
            part = slice(start, start + step)
            ug = (nt(lg_ref[...], down_s[s, part, :]) * slope_ref[s, :, part]).astype(bf16)
            ug_ref[s, :, part] = ug
            sums.append(column(ug.astype(f32)))
            first_grad = first_grad + nt(ug, up_s[s, :, part])
        up_bias_grads.append(jnp.concatenate(sums, axis=1))

    normed = normed_ref[...]
    grad = first_grad * gain_ref[...]
    back = grad - row_mean(grad) - normed * row_mean(grad * normed)
    back = inv_ref[:, :1] * back
    back_ref[...] = back
    low = back.astype(bf16)
    ag_ref[...] = low
    sums = [
        column(low.astype(f32)), column(first_grad * normed), column(first_grad),
        some_ref[0:1], some_ref[1:2], some_ref[2:3],
    ]
    row = lax.broadcasted_iota(jnp.int32, (FEAT, depth), 0)
    block = jnp.zeros((FEAT, depth), f32)
    for index, value in enumerate(sums):
        block = jnp.where(row == 1 + index, value, block)
    for s in range(n_mp):
        vec_ref[s] = block.astype(bf16)
        vec_ref[s, 0:1, :local] = up_bias_grads[s].astype(bf16)

    run_all([copies[s][0] for s in range(n_mp)], "wait")
    for s in range(n_mp):
        plane = me_ref[0] ^ s
        grads = nt(out_s[s], low).astype(bf16)
        dctx_ref[plane, :width] = grads
        product = grads.astype(f32) * contexts[s][:width].astype(f32)
        rows = None
        for h in range(heads):
            delta = -jnp.sum(product[h * HEAD:(h + 1) * HEAD], axis=0, keepdims=True)
            piece = split_rows(delta, FEAT, own, 3 * h)
            rows = piece if rows is None else rows + piece
        dctx_ref[plane, width:] = rows.astype(bf16)


def weight_scratch(n_mp, packed, width, depth, local):
    return [
        pltpu.VMEM((n_mp, width, depth), bf16),
        pltpu.VMEM((n_mp, depth, local), bf16),
        pltpu.VMEM((n_mp, local, depth), bf16),
    ], pltpu.SemaphoreType.DMA((n_mp, 3, max(2 * packed, 1)))


def feed(me, n_mp, packed, splits, hidden, out_grad, contexts, weights, banks, biases, vectors):
    rows, depth = hidden.shape
    own = rows // n_mp
    width, local = weights[0].shape[0], weights[1].shape[1]
    vmem = pl.BlockSpec(memory_space=pltpu.VMEM)
    hbm = pl.BlockSpec(memory_space=pl.ANY)
    mine = pl.BlockSpec((own, depth), lambda i, me: (me[0], 0))
    shape = jax.ShapeDtypeStruct
    scratch, sems = weight_scratch(n_mp, packed, width, depth, local)
    return pl.pallas_call(
        functools.partial(feed_kernel, n_mp, packed, splits),
        grid_spec=pltpu.PrefetchScalarGridSpec(
            num_scalar_prefetch=1,
            grid=(1,),
            in_specs=[mine, mine]
            + [vmem] * n_mp
            + [hbm] * (3 + len(banks))
            + [vmem, vmem],
            out_specs=[vmem] * 9,
            scratch_shapes=scratch + [pltpu.VMEM((own, depth), f32), sems],
        ),
        out_shape=[
            shape((own, depth), bf16),
            shape((own, depth), bf16),
            shape((n_mp, own, local), bf16),
            shape((n_mp, own, local), bf16),
            shape((own, depth), bf16),
            shape((own, depth), f32),
            shape((own, LANES), f32),
            shape((own, depth), f32),
            shape((8, depth), f32),
        ],
        compiler_params=params("arbitrary"),
        cost_estimate=pl.CostEstimate(
            flops=8 * own * depth * local * n_mp,
            bytes_accessed=4 * depth * local * n_mp,
            transcendentals=2 * own * local * n_mp,
        ),
        name="feed",
    )(me, hidden, out_grad, *contexts, *weights, *banks, biases, vectors)


def feed_back(
    me, n_mp, packed, splits, contexts, weights, banks, slope, lg, normed, inv, second, some, gain
):
    own, depth = lg.shape
    width, local = weights[0].shape[0], weights[1].shape[1]
    vmem = pl.BlockSpec(memory_space=pltpu.VMEM)
    hbm = pl.BlockSpec(memory_space=pl.ANY)
    shape = jax.ShapeDtypeStruct
    scratch, sems = weight_scratch(n_mp, packed, width, depth, local)
    return pl.pallas_call(
        functools.partial(feed_back_kernel, n_mp, packed, splits),
        grid_spec=pltpu.PrefetchScalarGridSpec(
            num_scalar_prefetch=1,
            grid=(1,),
            in_specs=[vmem] * n_mp + [hbm] * (3 + len(banks)) + [vmem] * 7,
            out_specs=[vmem] * 5,
            scratch_shapes=scratch + [sems],
        ),
        out_shape=[
            shape((n_mp, own, local), bf16),
            shape((own, depth), bf16),
            shape((own, depth), f32),
            shape((n_mp, width + FEAT, own), bf16),
            shape((n_mp, FEAT, depth), bf16),
        ],
        compiler_params=params("arbitrary"),
        cost_estimate=pl.CostEstimate(
            flops=8 * own * depth * local * n_mp,
            bytes_accessed=4 * depth * local * n_mp,
            transcendentals=0,
        ),
        name="feed_back",
    )(me, *contexts, *weights, *banks, slope, lg, normed, inv, second, some, gain)


def weigh_kernel(shares, first_ref, act_ref, ug_ref, lg_ref, ctx_ref, ag_ref, vec_ref, *refs):
    out_ref = refs[-1]
    out_rows, up_rows, down_rows = shares
    outs = nn(ctx_ref[0], ag_ref[...]).astype(bf16)
    ups = tn(first_ref[...], ug_ref[0]).astype(bf16)
    downs = tn(act_ref[0], lg_ref[...]).astype(bf16)
    for d in range(out_ref.shape[0]):
        at = 0
        for value, extent in ((outs, out_rows), (ups, up_rows), (downs, down_rows)):
            out_ref[d, 0, at:at + extent] = value[d * extent:(d + 1) * extent]
            at += extent
        out_ref[d, 0, at:] = vec_ref[0]


def weigh(n_dp, width, start, step, first_low, act, ug, lg, ctx, ag, vec, after):
    own, depth = first_low.shape
    n_mp, _, local = act.shape
    shares = (width // n_dp, depth // n_dp, local // n_dp)
    total = sum(shares) + FEAT
    count = min(4, n_dp)
    planes = n_mp // step
    whole = lambda *shape: pl.BlockSpec(shape, lambda s, d: (0, 0))
    return pl.pallas_call(
        functools.partial(weigh_kernel, shares),
        grid=(planes, n_dp // count),
        in_specs=[
            pl.BlockSpec((own, count * shares[1]), lambda s, d: (0, d)),
            pl.BlockSpec((1, own, count * shares[2]), lambda s, d: (start + step * s, 0, d)),
            pl.BlockSpec((1, own, local), lambda s, d: (start + step * s, 0, 0)),
            whole(own, depth),
            pl.BlockSpec((1, count * shares[0], own), lambda s, d: (start + step * s, d, 0)),
            whole(own, depth),
            pl.BlockSpec((1, FEAT, depth), lambda s, d: (start + step * s, 0, 0)),
        ]
        + [pl.BlockSpec(memory_space=pl.ANY)] * len(after),
        out_specs=pl.BlockSpec((count, 1, total, depth), lambda s, d: (d, s, 0, 0)),
        out_shape=jax.ShapeDtypeStruct((n_dp, planes, total, depth), bf16),
        compiler_params=params("arbitrary", "arbitrary"),
        cost_estimate=pl.CostEstimate(
            flops=8 * own * depth * local * planes,
            bytes_accessed=4 * depth * local * planes,
            transcendentals=0,
        ),
        name="weigh",
    )(first_low, act, ug, lg, ctx, ag, vec, *after)


def input_kernel(n_mp, packed, first, me_ref, back_ref, own_ref, bank_ref, *refs):
    grads, (out_ref, weight_s, sems) = refs[:-3], refs[-3:]
    total_rows = own_ref.shape[0]
    copies = [pltpu.make_async_copy(own_ref, weight_s.at[0], sems.at[0, 0])]
    for s in range(1, n_mp):
        if packed:
            rows = total_rows // packed
            for d in range(packed):
                if first * 3 * HEAD <= d * rows < (first + len(grads)) * 3 * HEAD:
                    copies.append(
                        pltpu.make_async_copy(
                            bank_ref.at[d, s - 1],
                            weight_s.at[s, d * rows:(d + 1) * rows],
                            sems.at[s, d],
                        )
                    )
        else:
            copies.append(
                pltpu.make_async_copy(bank_ref.at[s - 1], weight_s.at[s], sems.at[s, 0])
            )
    for copy in copies:
        copy.start()
    for copy in copies:
        copy.wait()
    total = back_ref[...]
    for h, grad_ref in enumerate(grads):
        part = slice(3 * HEAD * (first + h), 3 * HEAD * (first + h + 1))
        for s in range(n_mp):
            total = total + tn(grad_ref[me_ref[0] ^ s], weight_s[s, part])
    out_ref[...] = total.astype(out_ref.dtype)


def input_gradient(me, n_mp, packed, first, back, own_weight, bank, grads, kind):
    vmem = pl.BlockSpec(memory_space=pltpu.VMEM)
    hbm = pl.BlockSpec(memory_space=pl.ANY)
    return pl.pallas_call(
        functools.partial(input_kernel, n_mp, packed, first),
        in_specs=[pl.BlockSpec(memory_space=pltpu.SMEM), vmem, hbm, hbm] + [vmem] * len(grads),
        out_specs=vmem,
        out_shape=jax.ShapeDtypeStruct(back.shape, kind),
        scratch_shapes=[
            pltpu.VMEM((n_mp,) + own_weight.shape, bf16),
            pltpu.SemaphoreType.DMA((n_mp, max(packed, 1))),
        ],
        compiler_params=pltpu.CompilerParams(vmem_limit_bytes=VMEM_LIMIT),
        cost_estimate=pl.CostEstimate(
            flops=2 * back.size * own_weight.shape[0] * n_mp,
            bytes_accessed=2 * own_weight.size * n_mp,
            transcendentals=0,
        ),
        name="input_gradient",
    )(me, back, own_weight, bank, *grads)


def line_kernel(count, me_ref, own_ref, *refs):
    ahead, behind = refs[:count - 1], refs[count - 1:2 * count - 2]
    out_ref, slots, sems = refs[2 * count - 2:]
    me = me_ref[0]
    for k in range(count):
        if k == 0:
            pltpu.make_async_copy(own_ref, slots.at[0], sems.at[0, 0]).start()
            continue

        @pl.when(me >= k)
        def _():
            pltpu.make_async_copy(ahead[k - 1], slots.at[k], sems.at[0, k]).start()

        @pl.when(me < k)
        def _():
            pltpu.make_async_copy(behind[count - k - 1], slots.at[k], sems.at[0, k]).start()

    outs = []
    for k in range(count):
        pltpu.make_async_copy(own_ref, slots.at[k], sems.at[0, k]).wait()
        place = lax.rem(me + count - k, count)
        outs.append(pltpu.make_async_copy(slots.at[k], out_ref.at[place], sems.at[1, k]))
        outs[-1].start()
    for copy in outs:
        copy.wait()


def join_line(me, value, ahead, behind):
    count = len(ahead) + 1
    hbm = pl.BlockSpec(memory_space=pl.ANY)
    return pl.pallas_call(
        functools.partial(line_kernel, count),
        in_specs=[pl.BlockSpec(memory_space=pltpu.SMEM)] + [hbm] * (2 * count - 1),
        out_specs=hbm,
        out_shape=jax.ShapeDtypeStruct((count,) + value.shape, value.dtype),
        scratch_shapes=[
            pltpu.VMEM((count,) + value.shape, value.dtype),
            pltpu.SemaphoreType.DMA((2, count)),
        ],
        compiler_params=pltpu.CompilerParams(vmem_limit_bytes=VMEM_LIMIT),
        name="join_line",
    )(me, value, *ahead, *behind)


def weigh_input_kernel(hidden_ref, *refs):
    out_ref = refs[-1]
    depth, width = hidden_ref.shape[1], out_ref.shape[2]
    heads = width // HEAD
    for i in range(3):
        grads = jnp.concatenate([refs[3 * h + i][...] for h in range(heads)])
        out_ref[i, :depth] = nn(grads, hidden_ref[...]).T.astype(bf16)
        total = jnp.sum(grads.astype(f32), axis=1, keepdims=True)
        total = jnp.broadcast_to(total, (width, LANES)).T[:FEAT]
        out_ref[i, depth:] = total.astype(bf16)


def weigh_input(hidden, parts):
    rows, depth = hidden.shape
    width = len(parts) * HEAD
    vmem = pl.BlockSpec(memory_space=pltpu.VMEM)
    return pl.pallas_call(
        weigh_input_kernel,
        in_specs=[vmem] * (1 + 3 * len(parts)),
        out_specs=vmem,
        out_shape=jax.ShapeDtypeStruct((3, depth + FEAT, width), bf16),
        compiler_params=pltpu.CompilerParams(vmem_limit_bytes=VMEM_LIMIT),
        cost_estimate=pl.CostEstimate(
            flops=6 * rows * depth * width, bytes_accessed=8 * rows * depth, transcendentals=0
        ),
        name="weigh_input",
    )(hidden, *[item for part in parts for item in part])


def unpack_kernel(in_ref, *out_refs):
    at = 0
    for out_ref in out_refs:
        rows = out_ref.shape[0]
        out_ref[...] = in_ref[0, at:at + rows].astype(f32)
        at += rows


def unpack(shares, parts):
    count, total, depth = shares.shape
    return pl.pallas_call(
        unpack_kernel,
        grid=(count,),
        in_specs=[pl.BlockSpec((1, total, depth), lambda i: (i, 0, 0))],
        out_specs=[pl.BlockSpec((rows, depth), lambda i: (i, 0)) for rows in parts],
        out_shape=[jax.ShapeDtypeStruct((count * rows, depth), f32) for rows in parts],
        compiler_params=params("arbitrary"),
        name="unpack",
    )(shares)


def weigh_plain(s, n_dp, first_low, act, ug, lg, context, ag, vec):
    depth = first_low.shape[1]
    parts = [nn(context, ag), tn(first_low, ug[s]), tn(act[s], lg)]
    parts = [item.astype(bf16).reshape(n_dp, -1, depth) for item in parts]
    parts.append(jnp.broadcast_to(vec[s][None], (n_dp, FEAT, depth)))
    return jnp.concatenate(parts, axis=1)


def cross(value, count, bits):
    return lax.ppermute(value, "mp", [(i, i ^ bits) for i in range(count)])


def tie(values, others):
    return lax.optimization_barrier((values, others))[0]


def trade(value):
    return lax.all_to_all(value, "mp", 0, 0, tiled=True)


def swap(value, count, bit):
    return lax.ppermute(value, "dp", [(i, i ^ bit) for i in range(count)])


def hop(came, k, count):
    ahead, behind = came
    return (
        lax.ppermute(ahead, "mp", [(i, i + 1) for i in range(k - 1, count - 1)]),
        lax.ppermute(behind, "mp", [(i, i - 1) for i in range(1, count - k + 1)]),
    )


def finish_line(value, hops, me, count):
    while len(hops) < count - 1:
        hops = hops + [hop(hops[-1] if hops else (value, value), len(hops) + 1, count)]
    total = join_line(me, value, *zip(*hops))
    return total.reshape((-1,) + value.shape[1:])


def local(
    n_dp,
    n_mp,
    hidden,
    lengths,
    query_weight,
    query_bias,
    key_weight,
    key_bias,
    value_weight,
    value_bias,
    out_weight,
    out_bias,
    first_gain,
    first_shift,
    up_weight,
    up_bias,
    down_weight,
    down_bias,
    second_gain,
    second_shift,
    out_grad,
):
    rows, depth = hidden.shape
    width = query_weight.shape[1]
    hidden_local = up_weight.shape[1]
    heads = width // HEAD
    own = rows // n_mp
    me = lax.axis_index("mp")
    peer = lax.axis_index("dp")
    steps = range(n_mp)
    place = jnp.stack([me, peer]).astype(jnp.int32)

    def share_of(weight):
        share = weight.shape[0] // n_dp
        return lax.dynamic_slice_in_dim(weight, peer * share, share, 0)

    def gather_plane(value):
        return lax.all_gather(value, "dp", axis=0)

    def gather_others(weight):
        shares = [gather_plane(cross(share_of(weight), n_mp, s)) for s in steps if s]
        return jnp.stack([item.reshape(weight.shape) for item in shares])

    weights = [out_weight, up_weight, down_weight]
    qt, kt, kn, vt, vn, cosine, sine, turned = project(
        lengths, hidden, query_weight, key_weight, value_weight, query_bias, key_bias, value_bias
    )
    chips = n_dp // 2
    packed = n_dp if width // n_dp % FEAT == 0 and hidden_local == depth else 0
    splits = [1, n_mp - 1, n_mp] if n_mp > 2 else [1, n_mp]
    if packed:
        half = hidden_local // 2
        up_rows, down_rows, out_rows = depth // chips, half // chips, width // n_dp
        pack = make_pack(place, chips, up_weight, down_weight, out_weight, up_bias)
        marks = [up_rows, up_rows + 2 * (down_rows + out_rows)]
        crossed = {0: pack}
        for s in steps:
            if s & (s - 1) == 0 and s:
                crossed[s] = cross(pack, n_mp, s)
        bits = [2 << b for b in range(chips.bit_length() - 1)]

        def begin(group):
            group = jnp.stack([crossed[s] for s in group])[None]
            return [group[:, :, :marks[0]], group[:, :, marks[0]:marks[1]]]

        def double(held, step):
            came = [swap(held[0], n_dp, bits[step]), swap(held[1], n_dp, bits[-1 - step])]
            return came, lambda came: [jnp.concatenate(pair) for pair in zip(held, came)]

    contexts, tops, results = [None] * n_mp, [None] * n_mp, []

    def attend_next(after, count=1):
        first = n_mp - 1 - len(results)
        ctx, top = attend(place, first, count, n_mp, qt, kn, vt, after)
        for i in range(count):
            s = first - i
            tops[s] = top[i]
            results.append(ctx)
            contexts[s] = cross(ctx[i], n_mp, s) if s else ctx[i]

    if packed and n_mp == 4 and len(bits) == 2:
        attend_next([])
        crossed[1], crossed[2] = tie((crossed[1], crossed[2]), results[0])
        crossed[3] = cross(crossed[2], n_mp, 1)
        near = begin([1, 2])
        near_came, near_join = double(near, 0)
        attend_next([])
        near_came, crossed[3], contexts[3] = tie(
            (near_came, crossed[3], contexts[3]), results[1]
        )
        near = near_join(near_came)
        near_came, near_join = double(near, 1)
        far = begin([3])
        far_came, far_join = double(far, 0)
        attend_next([contexts[3]] + near + far, 2)
        near_came, far_came, contexts[2] = tie(
            (near_came, far_came, contexts[2]), results[3]
        )
        near, far = near_join(near_came), far_join(far_came)
        far_came, far_join = double(far, 1)
        near_other = [swap(item, n_dp, 1) for item in near]
        far = tie(far_join(far_came), contexts[1])
        banks = near + near_other + far + [swap(item, n_dp, 1) for item in far]
    else:
        for s in steps:
            attend_next([])
        if packed:
            banks = []
            for s in steps:
                if s & (s - 1):
                    crossed[s] = cross(crossed[s & (s - 1)], n_mp, s & -s)
            for i in range(len(splits) - 1):
                held = begin(range(splits[i], splits[i + 1]))
                for step in range(len(bits)):
                    came, join = double(held, step)
                    held = join(came)
                banks += held + [swap(item, n_dp, 1) for item in held]
    if packed:
        biases = [crossed[s][marks[1]:marks[1] + FEAT] for s in steps]
        biases = jnp.stack(
            [
                jnp.concatenate([jnp.sum(item[3 * c:3 * c + 3].astype(f32), 0) for c in range(2)])
                for item in biases
            ]
        )
    else:
        banks = [gather_others(item) for item in weights]
        biases = jnp.stack([up_bias] + [cross(up_bias, n_mp, s) for s in steps if s])
    tops = jnp.stack(tops)

    vectors = jnp.stack(
        [out_bias, first_gain, first_shift, down_bias, second_gain, second_shift]
    )
    result_own, first_low, act, slope, lg, normed, inv, second_back, some = feed(
        place, n_mp, packed, splits, hidden, out_grad, contexts, weights, banks, biases, vectors,
    )
    if packed:
        share = share_of(turned)
        shares = tie([cross(share, n_mp, s) for s in steps if s], lg)
        input_bank = gather_plane(jnp.stack(shares))
    else:
        input_bank = gather_others(turned)
    ug, ag, first_back, dctx, vec = feed_back(
        place, n_mp, packed, splits, contexts, weights, banks, slope, lg, normed, inv,
        second_back, some, first_gain[None],
    )
    came = tie(hop((result_own, result_own), 1, n_mp), lg if n_mp == 2 else ag)
    hops = [came]
    grads = trade(dctx)

    if packed:
        stacked = jnp.stack([item[:width] for item in contexts])
        operands = (first_low, act, ug, lg, stacked, ag, vec)
        odd = weigh(n_dp, width, 1, 2, *operands, list(came))
        even = weigh(n_dp, width, 0, 2, *operands, [grads])
        ready = [even]
        odd = lax.psum_scatter(tie(odd, (even, input_bank)), "dp", scatter_dimension=0, tiled=False)
        even = lax.psum_scatter(even, "dp", scatter_dimension=0, tiled=False)
    else:
        parts, ready = [], []
        for s in steps:
            part = weigh_plain(s, n_dp, first_low, act, ug, lg, contexts[s], ag, vec)
            parts.append(lax.psum_scatter(part, "dp", scatter_dimension=0, tiled=False))
        odd, even = jnp.stack(parts[1::2]), jnp.stack(parts[::2])

    parts, received = [], []
    for h in range(heads):
        after = ready if h == 0 else [came]
        after = jax.tree.leaves(after + [hops[0]]) if h == 0 else jax.tree.leaves(after)
        if h > 1:
            after.append(received[h - 2])
        *part, send = attend_back(
            place, h, n_mp, qt, kt, kn, vn, grads, tops, cosine, sine, after
        )
        if len(hops) < n_mp - 1:
            came = tie(hop(hops[-1], len(hops) + 1, n_mp), part[0])
            hops.append(came)
        elif h == n_mp - 2:
            came = odd = tie(cross(odd, n_mp, 1), part[0])
        parts.append(part)
        received.append(trade(tie(send, received[-1]) if h else send))
    if came is not odd:
        odd = cross(odd, n_mp, 1)
    result = finish_line(result_own, hops, place, n_mp)
    last = heads - 1
    sums_in = weigh_input(hidden, parts)
    input_grad = input_gradient(
        place, n_mp, packed, 0, tie(first_back, sums_in), turned, input_bank, received[:last], f32
    )
    hidden_own = input_gradient(
        place, n_mp, packed, last, input_grad, turned, input_bank, received[last:], bf16
    )
    first_hop = hop((hidden_own, hidden_own), 1, n_mp)
    even = tie(even, received[-1])
    input_sums = lax.psum(sums_in, "dp")
    tail = [first_hop]
    if n_mp > 2:
        tail.append(tie(hop(first_hop, 2, n_mp), input_sums))
    hidden_grad = finish_line(hidden_own, tail, place, n_mp)
    totals = [even[i].astype(f32) + odd[i].astype(f32) for i in range(n_mp // 2)]
    bit = 2
    while len(totals) > 1:
        sent = jnp.stack(totals[1::2]).astype(bf16)
        other = cross(sent, n_mp, bit)
        totals = [item + other[i].astype(f32) for i, item in enumerate(totals[::2])]
        bit *= 2
    total = totals[0]
    matrices = gather_plane(tie(total[:-FEAT].astype(bf16), first_hop))
    if packed:
        out_weight_grad, up_weight_grad, down_weight_grad = unpack(
            matrices, (width // n_dp, depth // n_dp, hidden_local // n_dp)
        )
    else:
        marks = [0, width, width + hidden_local, width + 2 * hidden_local]
        shapes = [(width, depth), (depth, hidden_local), (hidden_local, depth)]
        out_weight_grad, up_weight_grad, down_weight_grad = (
            matrices[:, marks[i] // n_dp:marks[i + 1] // n_dp].reshape(shapes[i]).astype(f32)
            for i in range(3)
        )
    sums = total[-FEAT:]
    input_sums = input_sums.astype(f32)
    input_grads = []
    for item in input_sums:
        input_grads += [item[:depth], item[depth]]
    return (
        result,
        hidden_grad,
        *input_grads,
        out_weight_grad,
        sums[1],
        sums[2],
        sums[3],
        up_weight_grad,
        sums[0, :hidden_local],
        down_weight_grad,
        sums[4],
        sums[5],
        sums[6],
    )


def solution(mesh):
    in_specs = (
        P("dp", None),
        P("dp", None),
        P(None, "mp"),
        P("mp"),
        P(None, "mp"),
        P("mp"),
        P(None, "mp"),
        P("mp"),
        P("mp", None),
        P(),
        P(),
        P(),
        P(None, "mp"),
        P("mp"),
        P("mp", None),
        P(),
        P(),
        P(),
        P("dp", None),
    )
    out_specs = (
        P("dp", None),
        P("dp", None),
        P(None, "mp"),
        P("mp"),
        P(None, "mp"),
        P("mp"),
        P(None, "mp"),
        P("mp"),
        P("mp", None),
        P(),
        P(),
        P(),
        P(None, "mp"),
        P("mp"),
        P("mp", None),
        P(),
        P(),
        P(),
    )
    body = functools.partial(local, mesh.shape["dp"], mesh.shape["mp"])
    return jax.shard_map(
        body, mesh=mesh, in_specs=in_specs, out_specs=out_specs, check_vma=False
    )
```

```python
import functools
import math

import jax
import jax.numpy as jnp
from jax import lax
from jax.experimental import pallas as pl
from jax.experimental.pallas import tpu as pltpu
from jax.sharding import PartitionSpec as P

HEAD = 64
HALF = HEAD // 2
LANES = 128
FEAT = 16
FAR = -1e30
FLOOR = -1e29
LOG2E = 1.4426950408889634
LN2 = 0.6931471805599453
VMEM_LIMIT = 60 * 1024 * 1024
epsilon = 1e-06
f32 = jnp.float32
bf16 = jnp.bfloat16


def params(*semantics):
    return pltpu.CompilerParams(
        dimension_semantics=semantics, vmem_limit_bytes=VMEM_LIMIT
    )


def nn(a, b):
    return lax.dot_general(a, b, (((1,), (0,)), ((), ())), preferred_element_type=f32)


def nt(a, b):
    return lax.dot_general(a, b, (((1,), (1,)), ((), ())), preferred_element_type=f32)


def tn(a, b):
    return lax.dot_general(a, b, (((0,), (0,)), ((), ())), preferred_element_type=f32)


def interleave_matrix(transposed):
    row = lax.broadcasted_iota(jnp.int32, (HEAD, HEAD), 0)
    col = lax.broadcasted_iota(jnp.int32, (HEAD, HEAD), 1)
    if transposed:
        row, col = col, row
    source = jnp.where(row < HALF, 2 * row, 2 * (row - HALF) + 1)
    return jnp.where(col == source, 1.0, 0.0).astype(bf16)


def project_kernel(
    heads, lengths_ref, hidden_ref, qw_ref, kw_ref, vw_ref, qb_ref, kb_ref, vb_ref,
    qt_ref, kt_ref, kn_ref, vt_ref, vn_ref, cos_ref, sin_ref, turned_ref, wt_ref, bias_ref,
):
    width = heads * HEAD
    rows = hidden_ref.shape[0]

    @pl.when(pl.program_id(0) == 0)
    def _():
        split = interleave_matrix(False)
        for index, weight in enumerate((qw_ref, kw_ref)):
            for h in range(heads):
                turned = weight[:, h * HEAD:(h + 1) * HEAD]
                wt_ref[index * width + h * HEAD:index * width + (h + 1) * HEAD, :] = nt(
                    split, turned
                ).astype(bf16)
        for index, weight in enumerate((qw_ref, kw_ref, vw_ref)):
            turned = weight[...].astype(f32).T.astype(bf16)
            for h in range(heads):
                at = (3 * h + index) * HEAD
                turned_ref[at:at + HEAD] = turned[h * HEAD:(h + 1) * HEAD]
        wt_ref[2 * width:, :] = turned
        same = jnp.where(
            lax.broadcasted_iota(jnp.int32, (HEAD, HEAD), 0)
            == lax.broadcasted_iota(jnp.int32, (HEAD, HEAD), 1),
            1.0,
            0.0,
        )
        chosen = (split.astype(f32), split.astype(f32), same)
        for index, source in enumerate((qb_ref, kb_ref, vb_ref)):
            for h in range(heads):
                part = source[:, h * HEAD:(h + 1) * HEAD]
                bias_ref[index * width + h * HEAD:index * width + (h + 1) * HEAD, :] = jnp.sum(
                    chosen[index] * part, axis=1, keepdims=True
                )

    token = lax.broadcasted_iota(jnp.int32, (8, rows), 1) + pl.program_id(0) * rows
    end = jnp.int32(0)
    segment = jnp.zeros((8, rows), jnp.int32)
    start = jnp.zeros((8, rows), jnp.int32)
    for j in range(lengths_ref.shape[1]):
        end = end + lengths_ref[0, j]
        past = token >= end
        segment = segment + past.astype(jnp.int32)
        start = jnp.where(past, jnp.maximum(start, end), start)
    valid = (token < end)[:1]
    segment = segment[:1]
    same = lax.broadcasted_iota(jnp.int32, (FEAT, rows), 0) == segment
    query_side = jnp.where(same, 1.0, 0.0).astype(bf16)
    key_side = jnp.where(same & valid, 0.0, FAR)
    position = (token - start)[:1].astype(f32)
    pair = lax.broadcasted_iota(jnp.int32, (HALF, rows), 0).astype(f32)
    angle = jnp.exp(pair * (-2.0 * math.log(10000.0) / HEAD)) * position
    cosine, sine = jnp.cos(angle), jnp.sin(angle)
    cos_ref[...] = cosine
    sin_ref[...] = sine
    lane_row = lax.broadcasted_iota(jnp.int32, (LANES - HEAD - FEAT, rows), 0)
    tail = jnp.where(lane_row < 3, 1.0, 0.0)
    ones_row = lax.broadcasted_iota(jnp.int32, (LANES - HEAD, rows), 0)
    projected = nt(wt_ref[...], hidden_ref[...]) + bias_ref[...]
    for h in range(heads):
        for index in range(2):
            base = index * width + h * HEAD
            former = projected[base:base + HALF]
            latter = projected[base + HALF:base + HEAD]
            turned_a = former * cosine - latter * sine
            turned_b = latter * cosine + former * sine
            if index == 0:
                scale = LOG2E / math.sqrt(HEAD)
                qt_ref[h] = jnp.concatenate(
                    [
                        (turned_a * scale).astype(bf16),
                        (turned_b * scale).astype(bf16),
                        query_side,
                        jnp.zeros((LANES - HEAD - FEAT, rows), bf16),
                    ],
                    axis=0,
                )
            else:
                kt_ref[h] = jnp.concatenate([turned_a, turned_b], axis=0).astype(bf16)
                kn_ref[h] = (
                    jnp.concatenate([turned_a, turned_b, key_side, tail], axis=0)
                    .T.astype(bf16)
                )
        base = 2 * width + h * HEAD
        flat = projected[base:base + HEAD]
        ones = jnp.where((ones_row >= 3 * h) & (ones_row < 3 * h + 3), 1.0, 0.0)
        vt_ref[h] = jnp.concatenate([flat, jnp.ones((FEAT, rows), f32)], axis=0).astype(bf16)
        vn_ref[h] = jnp.concatenate([flat, ones], axis=0).T.astype(bf16)


def project(lengths, hidden, qw, kw, vw, qb, kb, vb):
    rows, depth = hidden.shape
    width = qw.shape[1]
    heads = width // HEAD
    block = min(512, rows)
    whole = lambda *shape: pl.BlockSpec(shape, lambda i: (0,) * len(shape))
    table = pl.BlockSpec((HALF, block), lambda i: (0, i))
    return pl.pallas_call(
        functools.partial(project_kernel, heads),
        grid=(rows // block,),
        in_specs=[pl.BlockSpec(memory_space=pltpu.SMEM)]
        + [pl.BlockSpec((block, depth), lambda i: (i, 0))]
        + [whole(depth, width)] * 3
        + [whole(1, width)] * 3,
        out_specs=[
            pl.BlockSpec((heads, LANES, block), lambda i: (0, 0, i)),
            pl.BlockSpec((heads, HEAD, block), lambda i: (0, 0, i)),
            pl.BlockSpec((heads, block, LANES), lambda i: (0, i, 0)),
            pl.BlockSpec((heads, HEAD + FEAT, block), lambda i: (0, 0, i)),
            pl.BlockSpec((heads, block, LANES), lambda i: (0, i, 0)),
            table,
            table,
            whole(3 * width, depth),
        ],
        out_shape=[
            jax.ShapeDtypeStruct((heads, LANES, rows), bf16),
            jax.ShapeDtypeStruct((heads, HEAD, rows), bf16),
            jax.ShapeDtypeStruct((heads, rows, LANES), bf16),
            jax.ShapeDtypeStruct((heads, HEAD + FEAT, rows), bf16),
            jax.ShapeDtypeStruct((heads, rows, LANES), bf16),
            jax.ShapeDtypeStruct((HALF, rows), f32),
            jax.ShapeDtypeStruct((HALF, rows), f32),
            jax.ShapeDtypeStruct((3 * width, depth), bf16),
        ],
        scratch_shapes=[
            pltpu.VMEM((3 * width, depth), bf16), pltpu.VMEM((3 * width, 1), f32)
        ],
        compiler_params=params("arbitrary"),
        cost_estimate=pl.CostEstimate(
            flops=6 * rows * depth * width, bytes_accessed=16 * rows * depth, transcendentals=0
        ),
        name="project",
    )(lengths, hidden, qw, kw, vw, qb[None], kb[None], vb[None])


def pack_kernel(chips, me_ref, up_ref, down_ref, out_ref, bias_ref, pack_ref, sems):
    depth, local = up_ref.shape
    half, width = local // 2, out_ref.shape[0]
    core, chip = me_ref[1] & 1, me_ref[1] >> 1
    ups, downs, outs = depth // chips, half // chips, width // (2 * chips)
    row = pl.multiple_of(chip * ups, ups)
    pieces = [(up_ref, row, ups, pl.multiple_of(core * half, half))]
    row = pl.multiple_of(core * half + chip * downs, downs)
    pieces += [(down_ref, row, downs, c * half) for c in range(2)]
    row = pl.multiple_of(core * (width // 2) + chip * outs, outs)
    pieces += [(out_ref, row, outs, c * half) for c in range(2)]
    at, copies = 0, []
    for i, (source, row, extent, column) in enumerate(pieces):
        copies.append(
            pltpu.make_async_copy(
                source.at[pl.ds(row, extent), pl.ds(column, half)],
                pack_ref.at[at:at + extent],
                sems.at[i],
            )
        )
        at += extent
    for copy in copies:
        copy.start()
    row = lax.broadcasted_iota(jnp.int32, (FEAT, half), 0)
    total = jnp.zeros((FEAT, half), f32)
    for c in range(2):
        total = total + split_rows(bias_ref[:, c * half:(c + 1) * half], FEAT, half, 3 * c)
    pack_ref[at:] = total.astype(bf16)
    for copy in copies:
        copy.wait()


def make_pack(me, chips, up, down, out, bias):
    depth, local = up.shape
    half, width = local // 2, out.shape[0]
    rows = depth // chips + 2 * (half // chips + width // (2 * chips)) + FEAT
    hbm = pl.BlockSpec(memory_space=pl.ANY)
    vmem = pl.BlockSpec(memory_space=pltpu.VMEM)
    return pl.pallas_call(
        functools.partial(pack_kernel, chips),
        in_specs=[pl.BlockSpec(memory_space=pltpu.SMEM), hbm, hbm, hbm, vmem],
        out_specs=vmem,
        out_shape=jax.ShapeDtypeStruct((rows, half), bf16),
        scratch_shapes=[pltpu.SemaphoreType.DMA((5,))],
        name="pack",
    )(me, up, down, out, bias[None])


def attend_kernel(heads, me_ref, qt_ref, kn_ref, vt_ref, *refs):
    ctx_ref, lse_ref = refs[-2:]
    for h in range(heads):
        scores = nn(kn_ref[h], qt_ref[h])
        top = jnp.maximum(jnp.max(scores, axis=0, keepdims=True), FLOOR)
        weights = jnp.exp2(scores - top).astype(bf16)
        mixed = nn(vt_ref[h], weights)
        total = mixed[HEAD:HEAD + 1] + jnp.where(top <= FLOOR, 1.0, 0.0)
        ctx_ref[0, h * HEAD:(h + 1) * HEAD] = (mixed[:HEAD] / total).astype(bf16)
        lse_ref[0, h] = top + jnp.log2(total)


def attend(me, first, count, n_mp, qt, kn, vt, after):
    heads, _, rows = qt.shape
    own = rows // n_mp
    block = min(256, own)
    blocks = own // block
    whole = lambda *shape: pl.BlockSpec(shape, lambda i, me: (0,) * len(shape))
    return pl.pallas_call(
        functools.partial(attend_kernel, heads),
        grid_spec=pltpu.PrefetchScalarGridSpec(
            num_scalar_prefetch=1,
            grid=(count * blocks,),
            in_specs=[
                pl.BlockSpec(
                    (heads, LANES, block),
                    lambda i, me: (
                        0, 0, (me[0] ^ (first - i // blocks)) * blocks + i % blocks
                    ),
                ),
                whole(heads, rows, LANES),
                whole(heads, HEAD + FEAT, rows),
            ]
            + [pl.BlockSpec(memory_space=pl.ANY)] * len(after),
            out_specs=[
                pl.BlockSpec(
                    (1, heads * HEAD, block), lambda i, me: (i // blocks, 0, i % blocks)
                ),
                pl.BlockSpec(
                    (1, heads, 1, block), lambda i, me: (i // blocks, 0, 0, i % blocks)
                ),
            ],
        ),
        out_shape=[
            jax.ShapeDtypeStruct((count, heads * HEAD, own), bf16),
            jax.ShapeDtypeStruct((count, heads, 1, own), f32),
        ],
        compiler_params=params("arbitrary"),
        cost_estimate=pl.CostEstimate(
            flops=20 * heads * own * rows * HEAD * count,
            bytes_accessed=8 * rows * LANES * heads,
            transcendentals=heads * own * rows * count,
        ),
        name="attend",
    )(me, qt, kn, vt, *after)


def split_rows(value, count, rows, first):
    high = value.astype(bf16).astype(f32)
    rest = value - high
    middle = rest.astype(bf16).astype(f32)
    low = rest - middle
    row = lax.broadcasted_iota(jnp.int32, (count, rows), 0) - first
    return jnp.where(
        row == 0, high, jnp.where(row == 1, middle, jnp.where(row == 2, low, 0.0))
    )


def attend_back_kernel(
    chunk, me_ref, qt_ref, kt_ref, kn_ref, vn_ref, dot_ref, delta_ref, lse_ref, cosq_ref, sinq_ref,
    cos_ref, sin_ref, *refs,
):
    dq_ref, dk_ref, dv_ref, send_ref, dk_acc, dv_acc = refs[-6:]
    outer, inner = pl.program_id(0), pl.program_id(1)
    rows = kn_ref.shape[1]
    block = qt_ref.shape[2]
    query = qt_ref[0, :HEAD]
    grad = dot_ref[0]
    query_full = jnp.concatenate(
        [
            qt_ref[0, :HEAD + FEAT],
            split_rows(-lse_ref[0, 0], FEAT, block, 0).astype(bf16),
            jnp.zeros((LANES - HEAD - 2 * FEAT, block), bf16),
        ],
        axis=0,
    )
    grad_full = jnp.concatenate(
        [grad, delta_ref[0], jnp.zeros((LANES - HEAD - FEAT, block), bf16)], axis=0
    )

    @pl.when((outer == 0) & (inner == 0))
    def _():
        dk_acc[...] = jnp.zeros_like(dk_acc)
        dv_acc[...] = jnp.zeros_like(dv_acc)

    total = None
    for start in range(0, rows, chunk):
        part = slice(start, start + chunk)
        weights = jnp.exp2(nn(kn_ref[0, part], query_full))
        slopes = nn(vn_ref[0, part], grad_full)
        score_grad = (weights * slopes).astype(bf16)
        dv_acc[:, part] += nt(grad, weights.astype(bf16))
        dk_acc[:, part] += nt(query, score_grad)
        piece = nn(kt_ref[0, :, part], score_grad)
        total = piece if total is None else total + piece
    merge = interleave_matrix(True)

    def turn_back(value, cosine, sine, scale):
        former = value[:HALF] * scale
        latter = value[HALF:] * scale
        turned = jnp.concatenate(
            [former * cosine + latter * sine, latter * cosine - former * sine], axis=0
        )
        return nn(merge, turned.astype(bf16)).astype(bf16)

    dq = turn_back(total, cosq_ref[...], sinq_ref[...], 1.0 / math.sqrt(HEAD))
    dq_ref[...] = dq
    send_ref[outer, :HEAD, pl.ds(pl.multiple_of(inner * block, block), block)] = dq

    @pl.when((outer == pl.num_programs(0) - 1) & (inner == pl.num_programs(1) - 1))
    def _():
        dk = turn_back(dk_acc[...], cos_ref[...], sin_ref[...], LN2)
        dv = dv_acc[...].astype(bf16)
        dk_ref[...] = dk
        dv_ref[...] = dv
        count, _, own = send_ref.shape
        for j in range(count):
            send_ref[j, HEAD:2 * HEAD] = dk[:, j * own:(j + 1) * own]
            send_ref[j, 2 * HEAD:] = dv[:, j * own:(j + 1) * own]


def attend_back(me, head, n_mp, qt, kt, kn, vn, grads, lse, cosine, sine, after):
    heads, _, rows = qt.shape
    width = heads * HEAD
    own = rows // n_mp
    block = min(256, own)
    blocks = own // block
    chunk = min(512, rows)
    place = lambda j, i: j * blocks + i
    by_head = lambda *shape: pl.BlockSpec((1,) + shape, lambda j, i, me: (head, 0, 0))
    whole = lambda *shape: pl.BlockSpec(shape, lambda j, i, me: (0,) * len(shape))
    here = lambda count: pl.BlockSpec((count, block), lambda j, i, me: (0, place(j, i)))
    return pl.pallas_call(
        functools.partial(attend_back_kernel, chunk),
        grid_spec=pltpu.PrefetchScalarGridSpec(
            num_scalar_prefetch=1,
            grid=(n_mp, blocks),
            in_specs=[
                pl.BlockSpec((1, LANES, block), lambda j, i, me: (head, 0, place(j, i))),
                by_head(HEAD, rows),
                by_head(rows, LANES),
                by_head(rows, LANES),
                pl.BlockSpec((1, HEAD, block), lambda j, i, me: (j, head, i)),
                pl.BlockSpec((1, FEAT, block), lambda j, i, me: (j, width // FEAT, i)),
                pl.BlockSpec((1, 1, 1, block), lambda j, i, me: (me[0] ^ j, head, 0, i)),
                here(HALF),
                here(HALF),
                whole(HALF, rows),
                whole(HALF, rows),
            ]
            + [pl.BlockSpec(memory_space=pl.ANY)] * len(after),
            out_specs=[
                here(HEAD), whole(HEAD, rows), whole(HEAD, rows), whole(n_mp, 3 * HEAD, own)
            ],
            scratch_shapes=[pltpu.VMEM((HEAD, rows), f32)] * 2,
        ),
        out_shape=[jax.ShapeDtypeStruct((HEAD, rows), bf16)] * 3
        + [jax.ShapeDtypeStruct((n_mp, 3 * HEAD, own), bf16)],
        compiler_params=params("arbitrary", "arbitrary"),
        cost_estimate=pl.CostEstimate(
            flops=80 * rows * rows * HEAD,
            bytes_accessed=8 * rows * LANES,
            transcendentals=rows * rows,
        ),
        name="attend_back",
    )(me, qt, kt, kn, vn, grads, grads, lse, cosine, sine, cosine, sine, *after)


def gelu_parts(value):
    cumulative = 0.5 * (1.0 + lax.erf(value * 0.7071067811865476))
    density = jnp.exp(-0.5 * value * value) * 0.3989422804014327
    return value * cumulative, cumulative + value * density


def row_mean(value):
    return jnp.mean(value, axis=-1, keepdims=True)


def plane_orders(count):
    bits = [1 << b for b in range(count.bit_length() - 1)]
    orders = []
    for sequence in (bits, bits[::-1]):
        held = [0]
        for bit in sequence:
            held = held + [r ^ bit for r in held]
        orders.append(held)
    return orders


def weight_copies(n_mp, packed, splits, me_ref, weights, banks, targets, sems):
    depth, local = weights[1].shape
    width = weights[0].shape[0]
    copies = [[[], [], []] for _ in range(n_mp)]
    for m, source in enumerate(weights):
        copies[0][m].append(
            pltpu.make_async_copy(source, targets[m].at[0], sems.at[0, m, 0])
        )
    for s in range(1, n_mp):
        if not packed:
            for m in range(3):
                copies[s][m].append(
                    pltpu.make_async_copy(
                        banks[m].at[s - 1], targets[m].at[s], sems.at[s, m, 0]
                    )
                )
            continue
        group = max(i for i in range(len(splits) - 1) if splits[i] <= s)
        member = s - splits[group]
        half, chips = local // 2, packed // 2
        ups, downs, outs = depth // chips, half // chips, width // packed
        orders = plane_orders(chips)
        for core in range(2):
            mine = (me_ref[1] & 1) ^ core
            for r in range(chips):
                for kind in range(2):
                    source = banks[4 * group + 2 * core + kind].at[r, member]
                    chip = (me_ref[1] >> 1) ^ orders[kind][r]
                    if kind == 0:
                        pieces = [(1, 0, ups, chip * ups, mine * half)]
                    else:
                        at = pl.multiple_of(mine * half + chip * downs, downs)
                        pieces = [(2, c * downs, downs, at, c * half) for c in range(2)]
                        at = mine * (width // 2) + chip * outs
                        pieces += [
                            (0, 2 * downs + c * outs, outs, at, c * half) for c in range(2)
                        ]
                    for m, start, extent, row, column in pieces:
                        row = pl.multiple_of(row, extent)
                        if m == 1:
                            column = pl.multiple_of(column, half)
                        copies[s][m].append(
                            pltpu.make_async_copy(
                                source.at[start:start + extent],
                                targets[m].at[s, pl.ds(row, extent), pl.ds(column, half)],
                                sems.at[s, m, len(copies[s][m])],
                            )
                        )
    return copies


def column(value):
    return jnp.sum(value, axis=0, keepdims=True)


def run_all(groups, action):
    for group in groups:
        for copy in group:
            getattr(copy, action)()


def feed_kernel(n_mp, packed, splits, me_ref, hidden_ref, cot_ref, *refs):
    refs = list(refs)
    take = lambda count: [refs.pop(0) for _ in range(count)]
    contexts = take(n_mp)
    weights = take(3)
    banks = take(4 * (len(splits) - 1) if packed else 3)
    bias_ref, vectors_ref = take(2)
    (
        result_ref, first_low_ref, act_ref, slope_ref, lg_ref, normed_ref, inv_ref, back_ref,
        vec_ref, out_s, up_s, down_s, first_s, act_s, slope_s, sems, out_sems,
    ) = refs
    depth, local = weights[1].shape
    own = hidden_ref.shape[0]
    width = weights[0].shape[0]
    step = min(512, local)
    copies = weight_copies(
        n_mp, packed, splits, me_ref, weights, banks, (out_s, up_s, down_s), sems
    )
    for m in range(3):
        run_all([copies[s][m] for s in range(n_mp)], "start")
    run_all([copies[s][0] for s in range(n_mp)], "wait")

    out_bias, first_gain, first_shift, down_bias, second_gain, second_shift = (
        vectors_ref[i:i + 1, :] for i in range(6)
    )
    summed = hidden_ref[...].astype(f32) + out_bias
    for s in range(n_mp):
        summed = summed + tn(contexts[s][:width], out_s[s])
    centered = summed - row_mean(summed)
    first_inv = lax.rsqrt(row_mean(centered * centered) + epsilon)
    inv_ref[...] = jnp.broadcast_to(first_inv, inv_ref.shape)
    normed = centered * first_inv
    normed_ref[...] = normed
    first = normed * first_gain + first_shift
    first_s[...] = first
    first_low_ref[...] = first.astype(bf16)

    lowered, stored = None, []
    for s in range(n_mp):
        run_all(copies[s][1:], "wait")
        for start in range(0, local, step):
            part = slice(start, start + step)
            upper = nn(first_low_ref[...], up_s[s, :, part]) + bias_ref[s:s + 1, part]
            value, slope = gelu_parts(upper)
            act = value.astype(bf16)
            act_s[s, :, part] = act
            slope_s[s, :, part] = slope.astype(bf16)
            piece = nn(act, down_s[s, part, :])
            lowered = piece if lowered is None else lowered + piece
        stored.append(
            [
                pltpu.make_async_copy(act_s.at[s], act_ref.at[s], out_sems.at[0, s]),
                pltpu.make_async_copy(slope_s.at[s], slope_ref.at[s], out_sems.at[1, s]),
            ]
        )
        run_all(stored[s:], "start")

    summed = first_s[...] + (lowered + down_bias)
    centered = summed - row_mean(summed)
    second_inv = lax.rsqrt(row_mean(centered * centered) + epsilon)
    normed = centered * second_inv
    result_ref[...] = (normed * second_gain + second_shift).astype(bf16)
    cotangent = cot_ref[...].astype(f32)
    grad = cotangent * second_gain
    back = second_inv * (grad - row_mean(grad) - normed * row_mean(grad * normed))
    back_ref[...] = back
    low = back.astype(bf16)
    lg_ref[...] = low
    vec_ref[0:1] = column(low.astype(f32))
    vec_ref[1:2] = column(cotangent * normed)
    vec_ref[2:3] = column(cotangent)
    run_all(stored, "wait")


def feed_back_kernel(n_mp, packed, splits, me_ref, *refs):
    refs = list(refs)
    take = lambda count: [refs.pop(0) for _ in range(count)]
    contexts = take(n_mp)
    weights = take(3)
    banks = take(4 * (len(splits) - 1) if packed else 3)
    slope_ref, lg_ref, normed_ref, inv_ref, second_ref, some_ref, gain_ref = take(7)
    (
        ug_ref, ag_ref, back_ref, dctx_ref, vec_ref, out_s, up_s, down_s, slope_s, ug_s,
        normed_s, sems, more_sems,
    ) = refs
    depth, local = weights[1].shape
    own = lg_ref.shape[0]
    width = weights[0].shape[0]
    heads = width // HEAD
    step = min(512, local)
    copies = weight_copies(
        n_mp, packed, splits, me_ref, weights, banks, (out_s, up_s, down_s), sems
    )
    slopes = [
        pltpu.make_async_copy(slope_ref.at[s], slope_s.at[s], more_sems.at[0, s])
        for s in range(n_mp)
    ]
    stored = [
        pltpu.make_async_copy(ug_s.at[s], ug_ref.at[s], more_sems.at[1, s]) for s in range(n_mp)
    ]
    normed_copy = pltpu.make_async_copy(normed_ref, normed_s, more_sems.at[2, 0])
    for s in range(n_mp):
        copies[s][2].append(slopes[s])
        run_all(copies[s][:0:-1], "start")
    normed_copy.start()
    run_all([copies[s][0] for s in range(n_mp)], "start")

    first_grad = second_ref[...]
    up_bias_grads = []
    for s in range(n_mp):
        run_all(copies[s][:0:-1], "wait")
        sums = []
        for start in range(0, local, step):
            part = slice(start, start + step)
            ug = (nt(lg_ref[...], down_s[s, part, :]) * slope_s[s, :, part]).astype(bf16)
            ug_s[s, :, part] = ug
            sums.append(column(ug.astype(f32)))
            first_grad = first_grad + nt(ug, up_s[s, :, part])
        up_bias_grads.append(jnp.concatenate(sums, axis=1))
        stored[s].start()

    normed_copy.wait()
    normed = normed_s[...]
    grad = first_grad * gain_ref[...]
    back = grad - row_mean(grad) - normed * row_mean(grad * normed)
    back = inv_ref[:, :1] * back
    back_ref[...] = back
    low = back.astype(bf16)
    ag_ref[...] = low
    sums = [
        column(low.astype(f32)), column(first_grad * normed), column(first_grad),
        some_ref[0:1], some_ref[1:2], some_ref[2:3],
    ]
    row = lax.broadcasted_iota(jnp.int32, (FEAT, depth), 0)
    block = jnp.zeros((FEAT, depth), f32)
    for index, value in enumerate(sums):
        block = jnp.where(row == 1 + index, value, block)
    for s in range(n_mp):
        vec_ref[s] = block.astype(bf16)
        vec_ref[s, 0:1, :local] = up_bias_grads[s].astype(bf16)

    run_all([copies[s][0] for s in range(n_mp)], "wait")
    for s in range(n_mp):
        plane = me_ref[0] ^ s
        grads = nt(out_s[s], low).astype(bf16)
        dctx_ref[plane, :width] = grads
        product = grads.astype(f32) * contexts[s][:width].astype(f32)
        rows = None
        for h in range(heads):
            delta = -jnp.sum(product[h * HEAD:(h + 1) * HEAD], axis=0, keepdims=True)
            piece = split_rows(delta, FEAT, own, 3 * h)
            rows = piece if rows is None else rows + piece
        dctx_ref[plane, width:] = rows.astype(bf16)
    run_all([stored], "wait")


def weight_scratch(n_mp, packed, width, depth, local):
    return [
        pltpu.VMEM((n_mp, width, depth), bf16),
        pltpu.VMEM((n_mp, depth, local), bf16),
        pltpu.VMEM((n_mp, local, depth), bf16),
    ], pltpu.SemaphoreType.DMA((n_mp, 3, max(2 * packed, 1)))


def feed(me, n_mp, packed, splits, hidden, out_grad, contexts, weights, banks, biases, vectors):
    rows, depth = hidden.shape
    own = rows // n_mp
    width, local = weights[0].shape[0], weights[1].shape[1]
    vmem = pl.BlockSpec(memory_space=pltpu.VMEM)
    hbm = pl.BlockSpec(memory_space=pl.ANY)
    mine = pl.BlockSpec((own, depth), lambda i, me: (me[0], 0))
    shape = jax.ShapeDtypeStruct
    scratch, sems = weight_scratch(n_mp, packed, width, depth, local)
    return pl.pallas_call(
        functools.partial(feed_kernel, n_mp, packed, splits),
        grid_spec=pltpu.PrefetchScalarGridSpec(
            num_scalar_prefetch=1,
            grid=(1,),
            in_specs=[mine, mine]
            + [vmem] * n_mp
            + [hbm] * (3 + len(banks))
            + [vmem, vmem],
            out_specs=[vmem] * 2 + [hbm] * 2 + [vmem] * 5,
            scratch_shapes=scratch
            + [pltpu.VMEM((own, depth), f32)]
            + [pltpu.VMEM((n_mp, own, local), bf16)] * 2
            + [sems, pltpu.SemaphoreType.DMA((2, n_mp))],
        ),
        out_shape=[
            shape((own, depth), bf16),
            shape((own, depth), bf16),
            shape((n_mp, own, local), bf16),
            shape((n_mp, own, local), bf16),
            shape((own, depth), bf16),
            shape((own, depth), f32),
            shape((own, LANES), f32),
            shape((own, depth), f32),
            shape((8, depth), f32),
        ],
        compiler_params=params("arbitrary"),
        cost_estimate=pl.CostEstimate(
            flops=8 * own * depth * local * n_mp,
            bytes_accessed=4 * depth * local * n_mp,
            transcendentals=2 * own * local * n_mp,
        ),
        name="feed",
    )(me, hidden, out_grad, *contexts, *weights, *banks, biases, vectors)


def feed_back(
    me, n_mp, packed, splits, contexts, weights, banks, slope, lg, normed, inv, second, some, gain
):
    own, depth = lg.shape
    width, local = weights[0].shape[0], weights[1].shape[1]
    vmem = pl.BlockSpec(memory_space=pltpu.VMEM)
    hbm = pl.BlockSpec(memory_space=pl.ANY)
    shape = jax.ShapeDtypeStruct
    scratch, sems = weight_scratch(n_mp, packed, width, depth, local)
    return pl.pallas_call(
        functools.partial(feed_back_kernel, n_mp, packed, splits),
        grid_spec=pltpu.PrefetchScalarGridSpec(
            num_scalar_prefetch=1,
            grid=(1,),
            in_specs=[vmem] * n_mp
            + [hbm] * (3 + len(banks))
            + [hbm, vmem, hbm]
            + [vmem] * 4,
            out_specs=[hbm] + [vmem] * 4,
            scratch_shapes=scratch
            + [pltpu.VMEM((n_mp, own, local), bf16)] * 2
            + [pltpu.VMEM((own, depth), f32), sems, pltpu.SemaphoreType.DMA((3, n_mp))],
        ),
        out_shape=[
            shape((n_mp, own, local), bf16),
            shape((own, depth), bf16),
            shape((own, depth), f32),
            shape((n_mp, width + FEAT, own), bf16),
            shape((n_mp, FEAT, depth), bf16),
        ],
        compiler_params=params("arbitrary"),
        cost_estimate=pl.CostEstimate(
            flops=8 * own * depth * local * n_mp,
            bytes_accessed=4 * depth * local * n_mp,
            transcendentals=0,
        ),
        name="feed_back",
    )(me, *contexts, *weights, *banks, slope, lg, normed, inv, second, some, gain)


def weigh_kernel(shares, first_ref, act_ref, ug_ref, lg_ref, ctx_ref, ag_ref, vec_ref, *refs):
    out_ref = refs[-1]
    out_rows, up_rows, down_rows = shares
    outs = nn(ctx_ref[0], ag_ref[...]).astype(bf16)
    ups = tn(first_ref[...], ug_ref[0]).astype(bf16)
    downs = tn(act_ref[0], lg_ref[...]).astype(bf16)
    for d in range(out_ref.shape[0]):
        at = 0
        for value, extent in ((outs, out_rows), (ups, up_rows), (downs, down_rows)):
            out_ref[d, 0, at:at + extent] = value[d * extent:(d + 1) * extent]
            at += extent
        out_ref[d, 0, at:] = vec_ref[0]


def weigh(n_dp, width, start, step, first_low, act, ug, lg, ctx, ag, vec, after):
    own, depth = first_low.shape
    n_mp, _, local = act.shape
    shares = (width // n_dp, depth // n_dp, local // n_dp)
    total = sum(shares) + FEAT
    count = min(4, n_dp)
    planes = n_mp // step
    whole = lambda *shape: pl.BlockSpec(shape, lambda s, d: (0, 0))
    return pl.pallas_call(
        functools.partial(weigh_kernel, shares),
        grid=(planes, n_dp // count),
        in_specs=[
            pl.BlockSpec((own, count * shares[1]), lambda s, d: (0, d)),
            pl.BlockSpec((1, own, count * shares[2]), lambda s, d: (start + step * s, 0, d)),
            pl.BlockSpec((1, own, local), lambda s, d: (start + step * s, 0, 0)),
            whole(own, depth),
            pl.BlockSpec((1, count * shares[0], own), lambda s, d: (start + step * s, d, 0)),
            whole(own, depth),
            pl.BlockSpec((1, FEAT, depth), lambda s, d: (start + step * s, 0, 0)),
        ]
        + [pl.BlockSpec(memory_space=pl.ANY)] * len(after),
        out_specs=pl.BlockSpec((count, 1, total, depth), lambda s, d: (d, s, 0, 0)),
        out_shape=jax.ShapeDtypeStruct((n_dp, planes, total, depth), bf16),
        compiler_params=params("arbitrary", "arbitrary"),
        cost_estimate=pl.CostEstimate(
            flops=8 * own * depth * local * planes,
            bytes_accessed=4 * depth * local * planes,
            transcendentals=0,
        ),
        name="weigh",
    )(first_low, act, ug, lg, ctx, ag, vec, *after)


def input_kernel(n_mp, packed, first, me_ref, back_ref, own_ref, bank_ref, *refs):
    grads, (out_ref, weight_s, sems) = refs[:-3], refs[-3:]
    total_rows = own_ref.shape[0]
    copies = [pltpu.make_async_copy(own_ref, weight_s.at[0], sems.at[0, 0])]
    for s in range(1, n_mp):
        if packed:
            rows = total_rows // packed
            for d in range(packed):
                if first * 3 * HEAD <= d * rows < (first + len(grads)) * 3 * HEAD:
                    copies.append(
                        pltpu.make_async_copy(
                            bank_ref.at[d, s - 1],
                            weight_s.at[s, d * rows:(d + 1) * rows],
                            sems.at[s, d],
                        )
                    )
        else:
            copies.append(
                pltpu.make_async_copy(bank_ref.at[s - 1], weight_s.at[s], sems.at[s, 0])
            )
    for copy in copies:
        copy.start()
    for copy in copies:
        copy.wait()
    total = back_ref[...]
    for h, grad_ref in enumerate(grads):
        part = slice(3 * HEAD * (first + h), 3 * HEAD * (first + h + 1))
        for s in range(n_mp):
            total = total + tn(grad_ref[me_ref[0] ^ s], weight_s[s, part])
    out_ref[...] = total.astype(out_ref.dtype)


def input_gradient(me, n_mp, packed, first, back, own_weight, bank, grads, kind):
    vmem = pl.BlockSpec(memory_space=pltpu.VMEM)
    hbm = pl.BlockSpec(memory_space=pl.ANY)
    return pl.pallas_call(
        functools.partial(input_kernel, n_mp, packed, first),
        in_specs=[pl.BlockSpec(memory_space=pltpu.SMEM), vmem, hbm, hbm] + [vmem] * len(grads),
        out_specs=vmem,
        out_shape=jax.ShapeDtypeStruct(back.shape, kind),
        scratch_shapes=[
            pltpu.VMEM((n_mp,) + own_weight.shape, bf16),
            pltpu.SemaphoreType.DMA((n_mp, max(packed, 1))),
        ],
        compiler_params=pltpu.CompilerParams(vmem_limit_bytes=VMEM_LIMIT),
        cost_estimate=pl.CostEstimate(
            flops=2 * back.size * own_weight.shape[0] * n_mp,
            bytes_accessed=2 * own_weight.size * n_mp,
            transcendentals=0,
        ),
        name="input_gradient",
    )(me, back, own_weight, bank, *grads)


def line_kernel(count, me_ref, own_ref, *refs):
    ahead, behind = refs[:count - 1], refs[count - 1:2 * count - 2]
    out_ref, slots, sems = refs[2 * count - 2:]
    me = me_ref[0]
    for k in range(count):
        if k == 0:
            pltpu.make_async_copy(own_ref, slots.at[0], sems.at[0, 0]).start()
            continue

        @pl.when(me >= k)
        def _():
            pltpu.make_async_copy(ahead[k - 1], slots.at[k], sems.at[0, k]).start()

        @pl.when(me < k)
        def _():
            pltpu.make_async_copy(behind[count - k - 1], slots.at[k], sems.at[0, k]).start()

    outs = []
    for k in range(count):
        pltpu.make_async_copy(own_ref, slots.at[k], sems.at[0, k]).wait()
        place = lax.rem(me + count - k, count)
        outs.append(pltpu.make_async_copy(slots.at[k], out_ref.at[place], sems.at[1, k]))
        outs[-1].start()
    for copy in outs:
        copy.wait()


def join_line(me, value, ahead, behind):
    count = len(ahead) + 1
    hbm = pl.BlockSpec(memory_space=pl.ANY)
    return pl.pallas_call(
        functools.partial(line_kernel, count),
        in_specs=[pl.BlockSpec(memory_space=pltpu.SMEM)] + [hbm] * (2 * count - 1),
        out_specs=hbm,
        out_shape=jax.ShapeDtypeStruct((count,) + value.shape, value.dtype),
        scratch_shapes=[
            pltpu.VMEM((count,) + value.shape, value.dtype),
            pltpu.SemaphoreType.DMA((2, count)),
        ],
        compiler_params=pltpu.CompilerParams(vmem_limit_bytes=VMEM_LIMIT),
        name="join_line",
    )(me, value, *ahead, *behind)


def weigh_input_kernel(hidden_ref, *refs):
    out_ref = refs[-1]
    depth, width = hidden_ref.shape[1], out_ref.shape[2]
    heads = width // HEAD
    for i in range(3):
        grads = jnp.concatenate([refs[3 * h + i][...] for h in range(heads)])
        out_ref[i, :depth] = nn(grads, hidden_ref[...]).T.astype(bf16)
        total = jnp.sum(grads.astype(f32), axis=1, keepdims=True)
        total = jnp.broadcast_to(total, (width, LANES)).T[:FEAT]
        out_ref[i, depth:] = total.astype(bf16)


def weigh_input(hidden, parts):
    rows, depth = hidden.shape
    width = len(parts) * HEAD
    vmem = pl.BlockSpec(memory_space=pltpu.VMEM)
    return pl.pallas_call(
        weigh_input_kernel,
        in_specs=[vmem] * (1 + 3 * len(parts)),
        out_specs=vmem,
        out_shape=jax.ShapeDtypeStruct((3, depth + FEAT, width), bf16),
        compiler_params=pltpu.CompilerParams(vmem_limit_bytes=VMEM_LIMIT),
        cost_estimate=pl.CostEstimate(
            flops=6 * rows * depth * width, bytes_accessed=8 * rows * depth, transcendentals=0
        ),
        name="weigh_input",
    )(hidden, *[item for part in parts for item in part])


def unpack_kernel(in_ref, *out_refs):
    at = 0
    for out_ref in out_refs:
        rows = out_ref.shape[0]
        out_ref[...] = in_ref[0, at:at + rows].astype(f32)
        at += rows


def unpack(shares, parts):
    count, total, depth = shares.shape
    return pl.pallas_call(
        unpack_kernel,
        grid=(count,),
        in_specs=[pl.BlockSpec((1, total, depth), lambda i: (i, 0, 0))],
        out_specs=[pl.BlockSpec((rows, depth), lambda i: (i, 0)) for rows in parts],
        out_shape=[jax.ShapeDtypeStruct((count * rows, depth), f32) for rows in parts],
        compiler_params=params("arbitrary"),
        name="unpack",
    )(shares)


def weigh_plain(s, n_dp, first_low, act, ug, lg, context, ag, vec):
    depth = first_low.shape[1]
    parts = [nn(context, ag), tn(first_low, ug[s]), tn(act[s], lg)]
    parts = [item.astype(bf16).reshape(n_dp, -1, depth) for item in parts]
    parts.append(jnp.broadcast_to(vec[s][None], (n_dp, FEAT, depth)))
    return jnp.concatenate(parts, axis=1)


def cross(value, count, bits):
    return lax.ppermute(value, "mp", [(i, i ^ bits) for i in range(count)])


def tie(values, others):
    return lax.optimization_barrier((values, others))[0]


def trade(value):
    return lax.all_to_all(value, "mp", 0, 0, tiled=True)


def swap(value, count, bit):
    return lax.ppermute(value, "dp", [(i, i ^ bit) for i in range(count)])


def hop(came, k, count):
    ahead, behind = came
    return (
        lax.ppermute(ahead, "mp", [(i, i + 1) for i in range(k - 1, count - 1)]),
        lax.ppermute(behind, "mp", [(i, i - 1) for i in range(1, count - k + 1)]),
    )


def finish_line(value, hops, me, count):
    while len(hops) < count - 1:
        hops = hops + [hop(hops[-1] if hops else (value, value), len(hops) + 1, count)]
    total = join_line(me, value, *zip(*hops))
    return total.reshape((-1,) + value.shape[1:])


def local(
    n_dp,
    n_mp,
    hidden,
    lengths,
    query_weight,
    query_bias,
    key_weight,
    key_bias,
    value_weight,
    value_bias,
    out_weight,
    out_bias,
    first_gain,
    first_shift,
    up_weight,
    up_bias,
    down_weight,
    down_bias,
    second_gain,
    second_shift,
    out_grad,
):
    rows, depth = hidden.shape
    width = query_weight.shape[1]
    hidden_local = up_weight.shape[1]
    heads = width // HEAD
    own = rows // n_mp
    me = lax.axis_index("mp")
    peer = lax.axis_index("dp")
    steps = range(n_mp)
    place = jnp.stack([me, peer]).astype(jnp.int32)

    def share_of(weight):
        share = weight.shape[0] // n_dp
        return lax.dynamic_slice_in_dim(weight, peer * share, share, 0)

    def gather_plane(value):
        return lax.all_gather(value, "dp", axis=0)

    def gather_others(weight):
        shares = [gather_plane(cross(share_of(weight), n_mp, s)) for s in steps if s]
        return jnp.stack([item.reshape(weight.shape) for item in shares])

    weights = [out_weight, up_weight, down_weight]
    qt, kt, kn, vt, vn, cosine, sine, turned = project(
        lengths, hidden, query_weight, key_weight, value_weight, query_bias, key_bias, value_bias
    )
    chips = n_dp // 2
    packed = n_dp if width // n_dp % FEAT == 0 and hidden_local == depth else 0
    splits = [1, n_mp - 1, n_mp] if n_mp > 2 else [1, n_mp]
    if packed:
        half = hidden_local // 2
        up_rows, down_rows, out_rows = depth // chips, half // chips, width // n_dp
        pack = make_pack(place, chips, up_weight, down_weight, out_weight, up_bias)
        marks = [up_rows, up_rows + 2 * (down_rows + out_rows)]
        crossed = {0: pack}
        for s in steps:
            if s & (s - 1) == 0 and s:
                crossed[s] = cross(pack, n_mp, s)
        bits = [2 << b for b in range(chips.bit_length() - 1)]

        def begin(group):
            group = jnp.stack([crossed[s] for s in group])[None]
            return [group[:, :, :marks[0]], group[:, :, marks[0]:marks[1]]]

        def double(held, step):
            came = [swap(held[0], n_dp, bits[step]), swap(held[1], n_dp, bits[-1 - step])]
            return came, lambda came: [jnp.concatenate(pair) for pair in zip(held, came)]

    contexts, tops, results = [None] * n_mp, [None] * n_mp, []

    def attend_next(after, count=1):
        first = n_mp - 1 - len(results)
        ctx, top = attend(place, first, count, n_mp, qt, kn, vt, after)
        for i in range(count):
            s = first - i
            tops[s] = top[i]
            results.append(ctx)
            contexts[s] = cross(ctx[i], n_mp, s) if s else ctx[i]

    if packed and n_mp == 4 and len(bits) == 2:
        attend_next([])
        crossed[1], crossed[2] = tie((crossed[1], crossed[2]), results[0])
        crossed[3] = cross(crossed[2], n_mp, 1)
        near = begin([1, 2])
        near_came, near_join = double(near, 0)
        attend_next([])
        near_came, crossed[3], contexts[3] = tie(
            (near_came, crossed[3], contexts[3]), results[1]
        )
        near = near_join(near_came)
        near_came, near_join = double(near, 1)
        far = begin([3])
        far_came, far_join = double(far, 0)
        attend_next([contexts[3]] + near + far, 2)
        near_came, far_came, contexts[2] = tie(
            (near_came, far_came, contexts[2]), results[3]
        )
        near, far = near_join(near_came), far_join(far_came)
        far_came, far_join = double(far, 1)
        near_other = [swap(item, n_dp, 1) for item in near]
        far = tie(far_join(far_came), contexts[1])
        banks = near + near_other + far + [swap(item, n_dp, 1) for item in far]
    else:
        for s in steps:
            attend_next([])
        if packed:
            banks = []
            for s in steps:
                if s & (s - 1):
                    crossed[s] = cross(crossed[s & (s - 1)], n_mp, s & -s)
            for i in range(len(splits) - 1):
                held = begin(range(splits[i], splits[i + 1]))
                for step in range(len(bits)):
                    came, join = double(held, step)
                    held = join(came)
                banks += held + [swap(item, n_dp, 1) for item in held]
    if packed:
        biases = [crossed[s][marks[1]:marks[1] + FEAT] for s in steps]
        biases = jnp.stack(
            [
                jnp.concatenate([jnp.sum(item[3 * c:3 * c + 3].astype(f32), 0) for c in range(2)])
                for item in biases
            ]
        )
    else:
        banks = [gather_others(item) for item in weights]
        biases = jnp.stack([up_bias] + [cross(up_bias, n_mp, s) for s in steps if s])
    tops = jnp.stack(tops)

    vectors = jnp.stack(
        [out_bias, first_gain, first_shift, down_bias, second_gain, second_shift]
    )
    result_own, first_low, act, slope, lg, normed, inv, second_back, some = feed(
        place, n_mp, packed, splits, hidden, out_grad, contexts, weights, banks, biases, vectors,
    )
    if packed:
        share = share_of(turned)
        shares = tie([cross(share, n_mp, s) for s in steps if s], lg)
        input_bank = gather_plane(jnp.stack(shares))
    else:
        input_bank = gather_others(turned)
    ug, ag, first_back, dctx, vec = feed_back(
        place, n_mp, packed, splits, contexts, weights, banks, slope, lg, normed, inv,
        second_back, some, first_gain[None],
    )
    came = tie(hop((result_own, result_own), 1, n_mp), lg if n_mp == 2 else ag)
    hops = [came]
    grads = trade(dctx)

    if packed:
        stacked = jnp.stack([item[:width] for item in contexts])
        operands = (first_low, act, ug, lg, stacked, ag, vec)
        odd = weigh(n_dp, width, 1, 2, *operands, list(came))
        even = weigh(n_dp, width, 0, 2, *operands, [grads])
        ready = [even]
        odd = lax.psum_scatter(tie(odd, (even, input_bank)), "dp", scatter_dimension=0, tiled=False)
        even = lax.psum_scatter(even, "dp", scatter_dimension=0, tiled=False)
    else:
        parts, ready = [], []
        for s in steps:
            part = weigh_plain(s, n_dp, first_low, act, ug, lg, contexts[s], ag, vec)
            parts.append(lax.psum_scatter(part, "dp", scatter_dimension=0, tiled=False))
        odd, even = jnp.stack(parts[1::2]), jnp.stack(parts[::2])

    parts, received = [], []
    for h in range(heads):
        after = ready if h == 0 else [came]
        after = jax.tree.leaves(after + [hops[0]]) if h == 0 else jax.tree.leaves(after)
        if h > 1:
            after.append(received[h - 2])
        *part, send = attend_back(
            place, h, n_mp, qt, kt, kn, vn, grads, tops, cosine, sine, after
        )
        if len(hops) < n_mp - 1:
            came = tie(hop(hops[-1], len(hops) + 1, n_mp), part[0])
            hops.append(came)
        else:
            came = []
        parts.append(part)
        received.append(trade(tie(send, received[-1]) if h else send))
    result = finish_line(result_own, hops, place, n_mp)
    last = heads - 1
    sums_in = weigh_input(hidden, parts)
    odd = tie(cross(tie(odd, parts[-1][0]), n_mp, 1), sums_in)
    input_grad = input_gradient(
        place, n_mp, packed, 0, tie(first_back, sums_in), turned, input_bank, received[:last], f32
    )
    hidden_own = input_gradient(
        place, n_mp, packed, last, input_grad, turned, input_bank, received[last:], bf16
    )
    first_hop = hop((hidden_own, hidden_own), 1, n_mp)
    even = tie(even, hidden_own)
    input_sums = lax.psum(sums_in, "dp")
    tail = [first_hop]
    if n_mp > 2:
        tail.append(tie(hop(first_hop, 2, n_mp), input_sums))
    hidden_grad = finish_line(hidden_own, tail, place, n_mp)
    totals = [even[i].astype(f32) + odd[i].astype(f32) for i in range(n_mp // 2)]
    bit = 2
    while len(totals) > 1:
        sent = jnp.stack(totals[1::2]).astype(bf16)
        other = cross(sent, n_mp, bit)
        totals = [item + other[i].astype(f32) for i, item in enumerate(totals[::2])]
        bit *= 2
    total = totals[0]
    matrices = gather_plane(tie(total[:-FEAT].astype(bf16), first_hop))
    if packed:
        out_weight_grad, up_weight_grad, down_weight_grad = unpack(
            matrices, (width // n_dp, depth // n_dp, hidden_local // n_dp)
        )
    else:
        marks = [0, width, width + hidden_local, width + 2 * hidden_local]
        shapes = [(width, depth), (depth, hidden_local), (hidden_local, depth)]
        out_weight_grad, up_weight_grad, down_weight_grad = (
            matrices[:, marks[i] // n_dp:marks[i + 1] // n_dp].reshape(shapes[i]).astype(f32)
            for i in range(3)
        )
    sums = total[-FEAT:]
    input_sums = input_sums.astype(f32)
    input_grads = []
    for item in input_sums:
        input_grads += [item[:depth], item[depth]]
    return (
        result,
        hidden_grad,
        *input_grads,
        out_weight_grad,
        sums[1],
        sums[2],
        sums[3],
        up_weight_grad,
        sums[0, :hidden_local],
        down_weight_grad,
        sums[4],
        sums[5],
        sums[6],
    )


def solution(mesh):
    in_specs = (
        P("dp", None),
        P("dp", None),
        P(None, "mp"),
        P("mp"),
        P(None, "mp"),
        P("mp"),
        P(None, "mp"),
        P("mp"),
        P("mp", None),
        P(),
        P(),
        P(),
        P(None, "mp"),
        P("mp"),
        P("mp", None),
        P(),
        P(),
        P(),
        P("dp", None),
    )
    out_specs = (
        P("dp", None),
        P("dp", None),
        P(None, "mp"),
        P("mp"),
        P(None, "mp"),
        P("mp"),
        P(None, "mp"),
        P("mp"),
        P("mp", None),
        P(),
        P(),
        P(),
        P(None, "mp"),
        P("mp"),
        P("mp", None),
        P(),
        P(),
        P(),
    )
    body = functools.partial(local, mesh.shape["dp"], mesh.shape["mp"])
    return jax.shard_map(
        body, mesh=mesh, in_specs=in_specs, out_specs=out_specs, check_vma=False
    )
```

```python
import functools
import math

import jax
import jax.numpy as jnp
from jax import lax
from jax.experimental import pallas as pl
from jax.experimental.pallas import tpu as pltpu
from jax.sharding import PartitionSpec as P

HEAD = 64
HALF = HEAD // 2
LANES = 128
FEAT = 16
FAR = -1e30
FLOOR = -1e29
LOG2E = 1.4426950408889634
LN2 = 0.6931471805599453
VMEM_LIMIT = 60 * 1024 * 1024
epsilon = 1e-06
f32 = jnp.float32
bf16 = jnp.bfloat16


def params(*semantics):
    return pltpu.CompilerParams(
        dimension_semantics=semantics, vmem_limit_bytes=VMEM_LIMIT
    )


def nn(a, b):
    return lax.dot_general(a, b, (((1,), (0,)), ((), ())), preferred_element_type=f32)


def nt(a, b):
    return lax.dot_general(a, b, (((1,), (1,)), ((), ())), preferred_element_type=f32)


def tn(a, b):
    return lax.dot_general(a, b, (((0,), (0,)), ((), ())), preferred_element_type=f32)


def interleave_matrix(transposed):
    row = lax.broadcasted_iota(jnp.int32, (HEAD, HEAD), 0)
    col = lax.broadcasted_iota(jnp.int32, (HEAD, HEAD), 1)
    if transposed:
        row, col = col, row
    source = jnp.where(row < HALF, 2 * row, 2 * (row - HALF) + 1)
    return jnp.where(col == source, 1.0, 0.0).astype(bf16)


def project_kernel(
    heads, lengths_ref, hidden_ref, qw_ref, kw_ref, vw_ref, qb_ref, kb_ref, vb_ref,
    qt_ref, kt_ref, kn_ref, vt_ref, vn_ref, cos_ref, sin_ref, turned_ref, wt_ref, bias_ref,
):
    width = heads * HEAD
    rows = hidden_ref.shape[0]

    @pl.when(pl.program_id(0) == 0)
    def _():
        split = interleave_matrix(False)
        for index, weight in enumerate((qw_ref, kw_ref)):
            for h in range(heads):
                turned = weight[:, h * HEAD:(h + 1) * HEAD]
                wt_ref[index * width + h * HEAD:index * width + (h + 1) * HEAD, :] = nt(
                    split, turned
                ).astype(bf16)
        for index, weight in enumerate((qw_ref, kw_ref, vw_ref)):
            turned = weight[...].astype(f32).T.astype(bf16)
            for h in range(heads):
                at = (3 * h + index) * HEAD
                turned_ref[at:at + HEAD] = turned[h * HEAD:(h + 1) * HEAD]
        wt_ref[2 * width:, :] = turned
        same = jnp.where(
            lax.broadcasted_iota(jnp.int32, (HEAD, HEAD), 0)
            == lax.broadcasted_iota(jnp.int32, (HEAD, HEAD), 1),
            1.0,
            0.0,
        )
        chosen = (split.astype(f32), split.astype(f32), same)
        for index, source in enumerate((qb_ref, kb_ref, vb_ref)):
            for h in range(heads):
                part = source[:, h * HEAD:(h + 1) * HEAD]
                bias_ref[index * width + h * HEAD:index * width + (h + 1) * HEAD, :] = jnp.sum(
                    chosen[index] * part, axis=1, keepdims=True
                )

    token = lax.broadcasted_iota(jnp.int32, (8, rows), 1) + pl.program_id(0) * rows
    end = jnp.int32(0)
    segment = jnp.zeros((8, rows), jnp.int32)
    start = jnp.zeros((8, rows), jnp.int32)
    for j in range(lengths_ref.shape[1]):
        end = end + lengths_ref[0, j]
        past = token >= end
        segment = segment + past.astype(jnp.int32)
        start = jnp.where(past, jnp.maximum(start, end), start)
    valid = (token < end)[:1]
    segment = segment[:1]
    same = lax.broadcasted_iota(jnp.int32, (FEAT, rows), 0) == segment
    query_side = jnp.where(same, 1.0, 0.0).astype(bf16)
    key_side = jnp.where(same & valid, 0.0, FAR)
    position = (token - start)[:1].astype(f32)
    pair = lax.broadcasted_iota(jnp.int32, (HALF, rows), 0).astype(f32)
    angle = jnp.exp(pair * (-2.0 * math.log(10000.0) / HEAD)) * position
    cosine, sine = jnp.cos(angle), jnp.sin(angle)
    cos_ref[...] = cosine
    sin_ref[...] = sine
    lane_row = lax.broadcasted_iota(jnp.int32, (LANES - HEAD - FEAT, rows), 0)
    tail = jnp.where(lane_row < 3, 1.0, 0.0)
    ones_row = lax.broadcasted_iota(jnp.int32, (LANES - HEAD, rows), 0)
    projected = nt(wt_ref[...], hidden_ref[...]) + bias_ref[...]
    for h in range(heads):
        for index in range(2):
            base = index * width + h * HEAD
            former = projected[base:base + HALF]
            latter = projected[base + HALF:base + HEAD]
            turned_a = former * cosine - latter * sine
            turned_b = latter * cosine + former * sine
            if index == 0:
                scale = LOG2E / math.sqrt(HEAD)
                qt_ref[h] = jnp.concatenate(
                    [
                        (turned_a * scale).astype(bf16),
                        (turned_b * scale).astype(bf16),
                        query_side,
                        jnp.zeros((LANES - HEAD - FEAT, rows), bf16),
                    ],
                    axis=0,
                )
            else:
                kt_ref[h] = jnp.concatenate([turned_a, turned_b], axis=0).astype(bf16)
                kn_ref[h] = (
                    jnp.concatenate([turned_a, turned_b, key_side, tail], axis=0)
                    .T.astype(bf16)
                )
        base = 2 * width + h * HEAD
        flat = projected[base:base + HEAD]
        ones = jnp.where((ones_row >= 3 * h) & (ones_row < 3 * h + 3), 1.0, 0.0)
        vt_ref[h] = jnp.concatenate([flat, jnp.ones((FEAT, rows), f32)], axis=0).astype(bf16)
        vn_ref[h] = jnp.concatenate([flat, ones], axis=0).T.astype(bf16)


def project(lengths, hidden, qw, kw, vw, qb, kb, vb):
    rows, depth = hidden.shape
    width = qw.shape[1]
    heads = width // HEAD
    block = min(512, rows)
    whole = lambda *shape: pl.BlockSpec(shape, lambda i: (0,) * len(shape))
    table = pl.BlockSpec((HALF, block), lambda i: (0, i))
    return pl.pallas_call(
        functools.partial(project_kernel, heads),
        grid=(rows // block,),
        in_specs=[pl.BlockSpec(memory_space=pltpu.SMEM)]
        + [pl.BlockSpec((block, depth), lambda i: (i, 0))]
        + [whole(depth, width)] * 3
        + [whole(1, width)] * 3,
        out_specs=[
            pl.BlockSpec((heads, LANES, block), lambda i: (0, 0, i)),
            pl.BlockSpec((heads, HEAD, block), lambda i: (0, 0, i)),
            pl.BlockSpec((heads, block, LANES), lambda i: (0, i, 0)),
            pl.BlockSpec((heads, HEAD + FEAT, block), lambda i: (0, 0, i)),
            pl.BlockSpec((heads, block, LANES), lambda i: (0, i, 0)),
            table,
            table,
            whole(3 * width, depth),
        ],
        out_shape=[
            jax.ShapeDtypeStruct((heads, LANES, rows), bf16),
            jax.ShapeDtypeStruct((heads, HEAD, rows), bf16),
            jax.ShapeDtypeStruct((heads, rows, LANES), bf16),
            jax.ShapeDtypeStruct((heads, HEAD + FEAT, rows), bf16),
            jax.ShapeDtypeStruct((heads, rows, LANES), bf16),
            jax.ShapeDtypeStruct((HALF, rows), f32),
            jax.ShapeDtypeStruct((HALF, rows), f32),
            jax.ShapeDtypeStruct((3 * width, depth), bf16),
        ],
        scratch_shapes=[
            pltpu.VMEM((3 * width, depth), bf16), pltpu.VMEM((3 * width, 1), f32)
        ],
        compiler_params=params("arbitrary"),
        cost_estimate=pl.CostEstimate(
            flops=6 * rows * depth * width, bytes_accessed=16 * rows * depth, transcendentals=0
        ),
        name="project",
    )(lengths, hidden, qw, kw, vw, qb[None], kb[None], vb[None])


def pack_kernel(chips, me_ref, up_ref, down_ref, out_ref, bias_ref, pack_ref, sems):
    depth, local = up_ref.shape
    half, width = local // 2, out_ref.shape[0]
    core, chip = me_ref[1] & 1, me_ref[1] >> 1
    ups, downs, outs = depth // chips, half // chips, width // (2 * chips)
    row = pl.multiple_of(chip * ups, ups)
    pieces = [(up_ref, row, ups, pl.multiple_of(core * half, half))]
    row = pl.multiple_of(core * half + chip * downs, downs)
    pieces += [(down_ref, row, downs, c * half) for c in range(2)]
    row = pl.multiple_of(core * (width // 2) + chip * outs, outs)
    pieces += [(out_ref, row, outs, c * half) for c in range(2)]
    at, copies = 0, []
    for i, (source, row, extent, column) in enumerate(pieces):
        copies.append(
            pltpu.make_async_copy(
                source.at[pl.ds(row, extent), pl.ds(column, half)],
                pack_ref.at[at:at + extent],
                sems.at[i],
            )
        )
        at += extent
    for copy in copies:
        copy.start()
    row = lax.broadcasted_iota(jnp.int32, (FEAT, half), 0)
    total = jnp.zeros((FEAT, half), f32)
    for c in range(2):
        total = total + split_rows(bias_ref[:, c * half:(c + 1) * half], FEAT, half, 3 * c)
    pack_ref[at:] = total.astype(bf16)
    for copy in copies:
        copy.wait()


def make_pack(me, chips, up, down, out, bias):
    depth, local = up.shape
    half, width = local // 2, out.shape[0]
    rows = depth // chips + 2 * (half // chips + width // (2 * chips)) + FEAT
    hbm = pl.BlockSpec(memory_space=pl.ANY)
    vmem = pl.BlockSpec(memory_space=pltpu.VMEM)
    return pl.pallas_call(
        functools.partial(pack_kernel, chips),
        in_specs=[pl.BlockSpec(memory_space=pltpu.SMEM), hbm, hbm, hbm, vmem],
        out_specs=vmem,
        out_shape=jax.ShapeDtypeStruct((rows, half), bf16),
        scratch_shapes=[pltpu.SemaphoreType.DMA((5,))],
        name="pack",
    )(me, up, down, out, bias[None])


def attend_kernel(heads, me_ref, qt_ref, kn_ref, vt_ref, *refs):
    ctx_ref, lse_ref = refs[-2:]
    for h in range(heads):
        scores = nn(kn_ref[h], qt_ref[h])
        top = jnp.maximum(jnp.max(scores, axis=0, keepdims=True), FLOOR)
        weights = jnp.exp2(scores - top).astype(bf16)
        mixed = nn(vt_ref[h], weights)
        total = mixed[HEAD:HEAD + 1] + jnp.where(top <= FLOOR, 1.0, 0.0)
        ctx_ref[0, h * HEAD:(h + 1) * HEAD] = (mixed[:HEAD] / total).astype(bf16)
        lse_ref[0, h] = top + jnp.log2(total)


def attend(me, first, count, n_mp, qt, kn, vt, after):
    heads, _, rows = qt.shape
    own = rows // n_mp
    block = min(256, own)
    blocks = own // block
    whole = lambda *shape: pl.BlockSpec(shape, lambda i, me: (0,) * len(shape))
    return pl.pallas_call(
        functools.partial(attend_kernel, heads),
        grid_spec=pltpu.PrefetchScalarGridSpec(
            num_scalar_prefetch=1,
            grid=(count * blocks,),
            in_specs=[
                pl.BlockSpec(
                    (heads, LANES, block),
                    lambda i, me: (
                        0, 0, (me[0] ^ (first - i // blocks)) * blocks + i % blocks
                    ),
                ),
                whole(heads, rows, LANES),
                whole(heads, HEAD + FEAT, rows),
            ]
            + [pl.BlockSpec(memory_space=pl.ANY)] * len(after),
            out_specs=[
                pl.BlockSpec(
                    (1, heads * HEAD, block), lambda i, me: (i // blocks, 0, i % blocks)
                ),
                pl.BlockSpec(
                    (1, heads, 1, block), lambda i, me: (i // blocks, 0, 0, i % blocks)
                ),
            ],
        ),
        out_shape=[
            jax.ShapeDtypeStruct((count, heads * HEAD, own), bf16),
            jax.ShapeDtypeStruct((count, heads, 1, own), f32),
        ],
        compiler_params=params("arbitrary"),
        cost_estimate=pl.CostEstimate(
            flops=20 * heads * own * rows * HEAD * count,
            bytes_accessed=8 * rows * LANES * heads,
            transcendentals=heads * own * rows * count,
        ),
        name="attend",
    )(me, qt, kn, vt, *after)


def split_rows(value, count, rows, first):
    high = value.astype(bf16).astype(f32)
    rest = value - high
    middle = rest.astype(bf16).astype(f32)
    low = rest - middle
    row = lax.broadcasted_iota(jnp.int32, (count, rows), 0) - first
    return jnp.where(
        row == 0, high, jnp.where(row == 1, middle, jnp.where(row == 2, low, 0.0))
    )


def attend_back_kernel(
    chunk, me_ref, qt_ref, kt_ref, kn_ref, vn_ref, dot_ref, delta_ref, lse_ref, cosq_ref, sinq_ref,
    cos_ref, sin_ref, *refs,
):
    dq_ref, dk_ref, dv_ref, send_ref, dk_acc, dv_acc = refs[-6:]
    outer, inner = pl.program_id(0), pl.program_id(1)
    rows = kn_ref.shape[1]
    block = qt_ref.shape[2]
    query = qt_ref[0, :HEAD]
    grad = dot_ref[0]
    query_full = jnp.concatenate(
        [
            qt_ref[0, :HEAD + FEAT],
            split_rows(-lse_ref[0, 0], FEAT, block, 0).astype(bf16),
            jnp.zeros((LANES - HEAD - 2 * FEAT, block), bf16),
        ],
        axis=0,
    )
    grad_full = jnp.concatenate(
        [grad, delta_ref[0], jnp.zeros((LANES - HEAD - FEAT, block), bf16)], axis=0
    )

    @pl.when((outer == 0) & (inner == 0))
    def _():
        dk_acc[...] = jnp.zeros_like(dk_acc)
        dv_acc[...] = jnp.zeros_like(dv_acc)

    total = None
    for start in range(0, rows, chunk):
        part = slice(start, start + chunk)
        weights = jnp.exp2(nn(kn_ref[0, part], query_full))
        slopes = nn(vn_ref[0, part], grad_full)
        score_grad = (weights * slopes).astype(bf16)
        dv_acc[:, part] += nt(grad, weights.astype(bf16))
        dk_acc[:, part] += nt(query, score_grad)
        piece = nn(kt_ref[0, :, part], score_grad)
        total = piece if total is None else total + piece
    merge = interleave_matrix(True)

    def turn_back(value, cosine, sine, scale):
        former = value[:HALF] * scale
        latter = value[HALF:] * scale
        turned = jnp.concatenate(
            [former * cosine + latter * sine, latter * cosine - former * sine], axis=0
        )
        return nn(merge, turned.astype(bf16)).astype(bf16)

    dq = turn_back(total, cosq_ref[...], sinq_ref[...], 1.0 / math.sqrt(HEAD))
    dq_ref[...] = dq
    send_ref[outer, :HEAD, pl.ds(pl.multiple_of(inner * block, block), block)] = dq

    @pl.when((outer == pl.num_programs(0) - 1) & (inner == pl.num_programs(1) - 1))
    def _():
        dk = turn_back(dk_acc[...], cos_ref[...], sin_ref[...], LN2)
        dv = dv_acc[...].astype(bf16)
        dk_ref[...] = dk
        dv_ref[...] = dv
        count, _, own = send_ref.shape
        for j in range(count):
            send_ref[j, HEAD:2 * HEAD] = dk[:, j * own:(j + 1) * own]
            send_ref[j, 2 * HEAD:] = dv[:, j * own:(j + 1) * own]


def attend_back(me, head, n_mp, qt, kt, kn, vn, grads, lse, cosine, sine, after):
    heads, _, rows = qt.shape
    width = heads * HEAD
    own = rows // n_mp
    block = min(256, own)
    blocks = own // block
    chunk = min(512, rows)
    place = lambda j, i: j * blocks + i
    by_head = lambda *shape: pl.BlockSpec((1,) + shape, lambda j, i, me: (head, 0, 0))
    whole = lambda *shape: pl.BlockSpec(shape, lambda j, i, me: (0,) * len(shape))
    here = lambda count: pl.BlockSpec((count, block), lambda j, i, me: (0, place(j, i)))
    return pl.pallas_call(
        functools.partial(attend_back_kernel, chunk),
        grid_spec=pltpu.PrefetchScalarGridSpec(
            num_scalar_prefetch=1,
            grid=(n_mp, blocks),
            in_specs=[
                pl.BlockSpec((1, LANES, block), lambda j, i, me: (head, 0, place(j, i))),
                by_head(HEAD, rows),
                by_head(rows, LANES),
                by_head(rows, LANES),
                pl.BlockSpec((1, HEAD, block), lambda j, i, me: (j, head, i)),
                pl.BlockSpec((1, FEAT, block), lambda j, i, me: (j, width // FEAT, i)),
                pl.BlockSpec((1, 1, 1, block), lambda j, i, me: (me[0] ^ j, head, 0, i)),
                here(HALF),
                here(HALF),
                whole(HALF, rows),
                whole(HALF, rows),
            ]
            + [pl.BlockSpec(memory_space=pl.ANY)] * len(after),
            out_specs=[
                here(HEAD), whole(HEAD, rows), whole(HEAD, rows), whole(n_mp, 3 * HEAD, own)
            ],
            scratch_shapes=[pltpu.VMEM((HEAD, rows), f32)] * 2,
        ),
        out_shape=[jax.ShapeDtypeStruct((HEAD, rows), bf16)] * 3
        + [jax.ShapeDtypeStruct((n_mp, 3 * HEAD, own), bf16)],
        compiler_params=params("arbitrary", "arbitrary"),
        cost_estimate=pl.CostEstimate(
            flops=80 * rows * rows * HEAD,
            bytes_accessed=8 * rows * LANES,
            transcendentals=rows * rows,
        ),
        name="attend_back",
    )(me, qt, kt, kn, vn, grads, grads, lse, cosine, sine, cosine, sine, *after)


def gelu_parts(value):
    cumulative = 0.5 * (1.0 + lax.erf(value * 0.7071067811865476))
    density = jnp.exp(-0.5 * value * value) * 0.3989422804014327
    return value * cumulative, cumulative + value * density


def row_mean(value):
    return jnp.mean(value, axis=-1, keepdims=True)


def plane_orders(count):
    bits = [1 << b for b in range(count.bit_length() - 1)]
    orders = []
    for sequence in (bits, bits[::-1]):
        held = [0]
        for bit in sequence:
            held = held + [r ^ bit for r in held]
        orders.append(held)
    return orders


def weight_copies(n_mp, packed, splits, me_ref, weights, banks, targets, sems):
    depth, local = weights[1].shape
    width = weights[0].shape[0]
    copies = [[[], [], []] for _ in range(n_mp)]
    for m, source in enumerate(weights):
        copies[0][m].append(
            pltpu.make_async_copy(source, targets[m].at[0], sems.at[0, m, 0])
        )
    for s in range(1, n_mp):
        if not packed:
            for m in range(3):
                copies[s][m].append(
                    pltpu.make_async_copy(
                        banks[m].at[s - 1], targets[m].at[s], sems.at[s, m, 0]
                    )
                )
            continue
        group = max(i for i in range(len(splits) - 1) if splits[i] <= s)
        member = s - splits[group]
        half, chips = local // 2, packed // 2
        ups, downs, outs = depth // chips, half // chips, width // packed
        orders = plane_orders(chips)
        for core in range(2):
            mine = (me_ref[1] & 1) ^ core
            for r in range(chips):
                for kind in range(2):
                    source = banks[4 * group + 2 * core + kind].at[r, member]
                    chip = (me_ref[1] >> 1) ^ orders[kind][r]
                    if kind == 0:
                        pieces = [(1, 0, ups, chip * ups, mine * half)]
                    else:
                        at = pl.multiple_of(mine * half + chip * downs, downs)
                        pieces = [(2, c * downs, downs, at, c * half) for c in range(2)]
                        at = mine * (width // 2) + chip * outs
                        pieces += [
                            (0, 2 * downs + c * outs, outs, at, c * half) for c in range(2)
                        ]
                    for m, start, extent, row, column in pieces:
                        row = pl.multiple_of(row, extent)
                        if m == 1:
                            column = pl.multiple_of(column, half)
                        copies[s][m].append(
                            pltpu.make_async_copy(
                                source.at[start:start + extent],
                                targets[m].at[s, pl.ds(row, extent), pl.ds(column, half)],
                                sems.at[s, m, len(copies[s][m])],
                            )
                        )
    return copies


def column(value):
    return jnp.sum(value, axis=0, keepdims=True)


def run_all(groups, action):
    for group in groups:
        for copy in group:
            getattr(copy, action)()


def feed_kernel(n_mp, packed, splits, me_ref, hidden_ref, cot_ref, *refs):
    refs = list(refs)
    take = lambda count: [refs.pop(0) for _ in range(count)]
    contexts = take(n_mp)
    weights = take(3)
    banks = take(4 * (len(splits) - 1) if packed else 3)
    bias_ref, vectors_ref = take(2)
    (
        result_ref, first_low_ref, act_ref, slope_ref, lg_ref, normed_ref, inv_ref, back_ref,
        vec_ref, out_s, up_s, down_s, first_s, sems,
    ) = refs
    depth, local = weights[1].shape
    own = hidden_ref.shape[0]
    width = weights[0].shape[0]
    step = min(512, local)
    copies = weight_copies(
        n_mp, packed, splits, me_ref, weights, banks, (out_s, up_s, down_s), sems
    )
    for m in range(3):
        run_all([copies[s][m] for s in range(n_mp)], "start")
    run_all([copies[s][0] for s in range(n_mp)], "wait")

    out_bias, first_gain, first_shift, down_bias, second_gain, second_shift = (
        vectors_ref[i:i + 1, :] for i in range(6)
    )
    summed = hidden_ref[...].astype(f32) + out_bias
    for s in range(n_mp):
        summed = summed + tn(contexts[s][:width], out_s[s])
    centered = summed - row_mean(summed)
    first_inv = lax.rsqrt(row_mean(centered * centered) + epsilon)
    inv_ref[...] = jnp.broadcast_to(first_inv, inv_ref.shape)
    normed = centered * first_inv
    normed_ref[...] = normed
    first = normed * first_gain + first_shift
    first_s[...] = first
    first_low_ref[...] = first.astype(bf16)

    lowered = None
    for s in range(n_mp):
        run_all(copies[s][1:], "wait")
        for start in range(0, local, step):
            part = slice(start, start + step)
            upper = nn(first_low_ref[...], up_s[s, :, part]) + bias_ref[s:s + 1, part]
            value, slope = gelu_parts(upper)
            act = value.astype(bf16)
            act_ref[s, :, part] = act
            slope_ref[s, :, part] = slope.astype(bf16)
            piece = nn(act, down_s[s, part, :])
            lowered = piece if lowered is None else lowered + piece

    summed = first_s[...] + (lowered + down_bias)
    centered = summed - row_mean(summed)
    second_inv = lax.rsqrt(row_mean(centered * centered) + epsilon)
    normed = centered * second_inv
    result_ref[...] = (normed * second_gain + second_shift).astype(bf16)
    cotangent = cot_ref[...].astype(f32)
    grad = cotangent * second_gain
    back = second_inv * (grad - row_mean(grad) - normed * row_mean(grad * normed))
    back_ref[...] = back
    low = back.astype(bf16)
    lg_ref[...] = low
    vec_ref[0:1] = column(low.astype(f32))
    vec_ref[1:2] = column(cotangent * normed)
    vec_ref[2:3] = column(cotangent)


def feed_back_kernel(n_mp, packed, splits, me_ref, *refs):
    refs = list(refs)
    take = lambda count: [refs.pop(0) for _ in range(count)]
    contexts = take(n_mp)
    weights = take(3)
    banks = take(4 * (len(splits) - 1) if packed else 3)
    slope_ref, lg_ref, normed_ref, inv_ref, second_ref, some_ref, gain_ref = take(7)
    ug_ref, ag_ref, back_ref, dctx_ref, vec_ref, out_s, up_s, down_s, sems = refs[-9:]
    depth, local = weights[1].shape
    own = lg_ref.shape[0]
    width = weights[0].shape[0]
    heads = width // HEAD
    step = min(512, local)
    copies = weight_copies(
        n_mp, packed, splits, me_ref, weights, banks, (out_s, up_s, down_s), sems
    )
    for s in range(n_mp):
        run_all(copies[s][:0:-1], "start")
    run_all([copies[s][0] for s in range(n_mp)], "start")

    first_grad = second_ref[...]
    up_bias_grads = []
    for s in range(n_mp):
        run_all(copies[s][:0:-1], "wait")
        sums = []
        for start in range(0, local, step):
            part = slice(start, start + step)
            ug = (nt(lg_ref[...], down_s[s, part, :]) * slope_ref[s, :, part]).astype(bf16)
            ug_ref[s, :, part] = ug
            sums.append(column(ug.astype(f32)))
            first_grad = first_grad + nt(ug, up_s[s, :, part])
        up_bias_grads.append(jnp.concatenate(sums, axis=1))

    normed = normed_ref[...]
    grad = first_grad * gain_ref[...]
    back = grad - row_mean(grad) - normed * row_mean(grad * normed)
    back = inv_ref[:, :1] * back
    back_ref[...] = back
    low = back.astype(bf16)
    ag_ref[...] = low
    sums = [
        column(low.astype(f32)), column(first_grad * normed), column(first_grad),
        some_ref[0:1], some_ref[1:2], some_ref[2:3],
    ]
    row = lax.broadcasted_iota(jnp.int32, (FEAT, depth), 0)
    block = jnp.zeros((FEAT, depth), f32)
    for index, value in enumerate(sums):
        block = jnp.where(row == 1 + index, value, block)
    for s in range(n_mp):
        vec_ref[s] = block.astype(bf16)
        vec_ref[s, 0:1, :local] = up_bias_grads[s].astype(bf16)

    run_all([copies[s][0] for s in range(n_mp)], "wait")
    for s in range(n_mp):
        plane = me_ref[0] ^ s
        grads = nt(out_s[s], low).astype(bf16)
        dctx_ref[plane, :width] = grads
        product = grads.astype(f32) * contexts[s][:width].astype(f32)
        rows = None
        for h in range(heads):
            delta = -jnp.sum(product[h * HEAD:(h + 1) * HEAD], axis=0, keepdims=True)
            piece = split_rows(delta, FEAT, own, 3 * h)
            rows = piece if rows is None else rows + piece
        dctx_ref[plane, width:] = rows.astype(bf16)


def weight_scratch(n_mp, packed, width, depth, local):
    return [
        pltpu.VMEM((n_mp, width, depth), bf16),
        pltpu.VMEM((n_mp, depth, local), bf16),
        pltpu.VMEM((n_mp, local, depth), bf16),
    ], pltpu.SemaphoreType.DMA((n_mp, 3, max(2 * packed, 1)))


def feed(me, n_mp, packed, splits, hidden, out_grad, contexts, weights, banks, biases, vectors):
    rows, depth = hidden.shape
    own = rows // n_mp
    width, local = weights[0].shape[0], weights[1].shape[1]
    vmem = pl.BlockSpec(memory_space=pltpu.VMEM)
    hbm = pl.BlockSpec(memory_space=pl.ANY)
    mine = pl.BlockSpec((own, depth), lambda i, me: (me[0], 0))
    shape = jax.ShapeDtypeStruct
    scratch, sems = weight_scratch(n_mp, packed, width, depth, local)
    return pl.pallas_call(
        functools.partial(feed_kernel, n_mp, packed, splits),
        grid_spec=pltpu.PrefetchScalarGridSpec(
            num_scalar_prefetch=1,
            grid=(1,),
            in_specs=[mine, mine]
            + [vmem] * n_mp
            + [hbm] * (3 + len(banks))
            + [vmem, vmem],
            out_specs=[vmem] * 9,
            scratch_shapes=scratch + [pltpu.VMEM((own, depth), f32), sems],
        ),
        out_shape=[
            shape((own, depth), bf16),
            shape((own, depth), bf16),
            shape((n_mp, own, local), bf16),
            shape((n_mp, own, local), bf16),
            shape((own, depth), bf16),
            shape((own, depth), f32),
            shape((own, LANES), f32),
            shape((own, depth), f32),
            shape((8, depth), f32),
        ],
        compiler_params=params("arbitrary"),
        cost_estimate=pl.CostEstimate(
            flops=8 * own * depth * local * n_mp,
            bytes_accessed=4 * depth * local * n_mp,
            transcendentals=2 * own * local * n_mp,
        ),
        name="feed",
    )(me, hidden, out_grad, *contexts, *weights, *banks, biases, vectors)


def feed_back(
    me, n_mp, packed, splits, contexts, weights, banks, slope, lg, normed, inv, second, some, gain
):
    own, depth = lg.shape
    width, local = weights[0].shape[0], weights[1].shape[1]
    vmem = pl.BlockSpec(memory_space=pltpu.VMEM)
    hbm = pl.BlockSpec(memory_space=pl.ANY)
    shape = jax.ShapeDtypeStruct
    scratch, sems = weight_scratch(n_mp, packed, width, depth, local)
    return pl.pallas_call(
        functools.partial(feed_back_kernel, n_mp, packed, splits),
        grid_spec=pltpu.PrefetchScalarGridSpec(
            num_scalar_prefetch=1,
            grid=(1,),
            in_specs=[vmem] * n_mp + [hbm] * (3 + len(banks)) + [vmem] * 7,
            out_specs=[vmem] * 5,
            scratch_shapes=scratch + [sems],
        ),
        out_shape=[
            shape((n_mp, own, local), bf16),
            shape((own, depth), bf16),
            shape((own, depth), f32),
            shape((n_mp, width + FEAT, own), bf16),
            shape((n_mp, FEAT, depth), bf16),
        ],
        compiler_params=params("arbitrary"),
        cost_estimate=pl.CostEstimate(
            flops=8 * own * depth * local * n_mp,
            bytes_accessed=4 * depth * local * n_mp,
            transcendentals=0,
        ),
        name="feed_back",
    )(me, *contexts, *weights, *banks, slope, lg, normed, inv, second, some, gain)


def weigh_kernel(shares, first_ref, act_ref, ug_ref, lg_ref, ctx_ref, ag_ref, vec_ref, *refs):
    out_ref = refs[-1]
    out_rows, up_rows, down_rows = shares
    outs = nn(ctx_ref[0], ag_ref[...]).astype(bf16)
    ups = tn(first_ref[...], ug_ref[0]).astype(bf16)
    downs = tn(act_ref[0], lg_ref[...]).astype(bf16)
    for d in range(out_ref.shape[0]):
        at = 0
        for value, extent in ((outs, out_rows), (ups, up_rows), (downs, down_rows)):
            out_ref[d, 0, at:at + extent] = value[d * extent:(d + 1) * extent]
            at += extent
        out_ref[d, 0, at:] = vec_ref[0]


def weigh(n_dp, width, start, planes, first_low, act, ug, lg, ctx, ag, vec, base, after):
    own, depth = first_low.shape
    n_mp, _, local = act.shape
    shares = (width // n_dp, depth // n_dp, local // n_dp)
    total = sum(shares) + FEAT
    count = min(4, n_dp)
    extra = ([] if base is None else [base]) + after
    whole = lambda *shape: pl.BlockSpec(shape, lambda s, d: (0, 0))
    return pl.pallas_call(
        functools.partial(weigh_kernel, shares),
        grid=(planes, n_dp // count),
        in_specs=[
            pl.BlockSpec((own, count * shares[1]), lambda s, d: (0, d)),
            pl.BlockSpec((1, own, count * shares[2]), lambda s, d: (start + s, 0, d)),
            pl.BlockSpec((1, own, local), lambda s, d: (start + s, 0, 0)),
            whole(own, depth),
            pl.BlockSpec((1, count * shares[0], own), lambda s, d: (start + s, d, 0)),
            whole(own, depth),
            pl.BlockSpec((1, FEAT, depth), lambda s, d: (start + s, 0, 0)),
        ]
        + [pl.BlockSpec(memory_space=pl.ANY)] * len(extra),
        out_specs=pl.BlockSpec((count, 1, total, depth), lambda s, d: (d, start + s, 0, 0)),
        out_shape=jax.ShapeDtypeStruct((n_dp, n_mp, total, depth), bf16),
        input_output_aliases={} if base is None else {7: 0},
        compiler_params=params("arbitrary", "arbitrary"),
        cost_estimate=pl.CostEstimate(
            flops=8 * own * depth * local * planes,
            bytes_accessed=4 * depth * local * planes,
            transcendentals=0,
        ),
        name="weigh",
    )(first_low, act, ug, lg, ctx, ag, vec, *extra)


def input_kernel(n_mp, packed, first, me_ref, back_ref, own_ref, bank_ref, *refs):
    grads, (out_ref, weight_s, sems) = refs[:-3], refs[-3:]
    total_rows = own_ref.shape[0]
    copies = [pltpu.make_async_copy(own_ref, weight_s.at[0], sems.at[0, 0])]
    for s in range(1, n_mp):
        if packed:
            rows = total_rows // packed
            for d in range(packed):
                if first * 3 * HEAD <= d * rows < (first + len(grads)) * 3 * HEAD:
                    copies.append(
                        pltpu.make_async_copy(
                            bank_ref.at[d, s - 1],
                            weight_s.at[s, d * rows:(d + 1) * rows],
                            sems.at[s, d],
                        )
                    )
        else:
            copies.append(
                pltpu.make_async_copy(bank_ref.at[s - 1], weight_s.at[s], sems.at[s, 0])
            )
    for copy in copies:
        copy.start()
    for copy in copies:
        copy.wait()
    total = back_ref[...]
    for h, grad_ref in enumerate(grads):
        part = slice(3 * HEAD * (first + h), 3 * HEAD * (first + h + 1))
        for s in range(n_mp):
            total = total + tn(grad_ref[me_ref[0] ^ s], weight_s[s, part])
    out_ref[...] = total.astype(out_ref.dtype)


def input_gradient(me, n_mp, packed, first, back, own_weight, bank, grads, kind):
    vmem = pl.BlockSpec(memory_space=pltpu.VMEM)
    hbm = pl.BlockSpec(memory_space=pl.ANY)
    return pl.pallas_call(
        functools.partial(input_kernel, n_mp, packed, first),
        in_specs=[pl.BlockSpec(memory_space=pltpu.SMEM), vmem, hbm, hbm] + [vmem] * len(grads),
        out_specs=vmem,
        out_shape=jax.ShapeDtypeStruct(back.shape, kind),
        scratch_shapes=[
            pltpu.VMEM((n_mp,) + own_weight.shape, bf16),
            pltpu.SemaphoreType.DMA((n_mp, max(packed, 1))),
        ],
        compiler_params=pltpu.CompilerParams(vmem_limit_bytes=VMEM_LIMIT),
        cost_estimate=pl.CostEstimate(
            flops=2 * back.size * own_weight.shape[0] * n_mp,
            bytes_accessed=2 * own_weight.size * n_mp,
            transcendentals=0,
        ),
        name="input_gradient",
    )(me, back, own_weight, bank, *grads)


def line_kernel(count, me_ref, own_ref, *refs):
    ahead, behind = refs[:count - 1], refs[count - 1:2 * count - 2]
    out_ref, slots, sems = refs[2 * count - 2:]
    me = me_ref[0]
    for k in range(count):
        if k == 0:
            pltpu.make_async_copy(own_ref, slots.at[0], sems.at[0, 0]).start()
            continue

        @pl.when(me >= k)
        def _():
            pltpu.make_async_copy(ahead[k - 1], slots.at[k], sems.at[0, k]).start()

        @pl.when(me < k)
        def _():
            pltpu.make_async_copy(behind[count - k - 1], slots.at[k], sems.at[0, k]).start()

    outs = []
    for k in range(count):
        pltpu.make_async_copy(own_ref, slots.at[k], sems.at[0, k]).wait()
        place = lax.rem(me + count - k, count)
        outs.append(pltpu.make_async_copy(slots.at[k], out_ref.at[place], sems.at[1, k]))
        outs[-1].start()
    for copy in outs:
        copy.wait()


def join_line(me, value, ahead, behind):
    count = len(ahead) + 1
    hbm = pl.BlockSpec(memory_space=pl.ANY)
    return pl.pallas_call(
        functools.partial(line_kernel, count),
        in_specs=[pl.BlockSpec(memory_space=pltpu.SMEM)] + [hbm] * (2 * count - 1),
        out_specs=hbm,
        out_shape=jax.ShapeDtypeStruct((count,) + value.shape, value.dtype),
        scratch_shapes=[
            pltpu.VMEM((count,) + value.shape, value.dtype),
            pltpu.SemaphoreType.DMA((2, count)),
        ],
        compiler_params=pltpu.CompilerParams(vmem_limit_bytes=VMEM_LIMIT),
        name="join_line",
    )(me, value, *ahead, *behind)


def weigh_input_kernel(hidden_ref, *refs):
    out_ref = refs[-1]
    depth, width = hidden_ref.shape[1], out_ref.shape[2]
    heads = width // HEAD
    for i in range(3):
        grads = jnp.concatenate([refs[3 * h + i][...] for h in range(heads)])
        out_ref[i, :depth] = nn(grads, hidden_ref[...]).T.astype(bf16)
        total = jnp.sum(grads.astype(f32), axis=1, keepdims=True)
        total = jnp.broadcast_to(total, (width, LANES)).T[:FEAT]
        out_ref[i, depth:] = total.astype(bf16)


def weigh_input(hidden, parts):
    rows, depth = hidden.shape
    width = len(parts) * HEAD
    vmem = pl.BlockSpec(memory_space=pltpu.VMEM)
    return pl.pallas_call(
        weigh_input_kernel,
        in_specs=[vmem] * (1 + 3 * len(parts)),
        out_specs=vmem,
        out_shape=jax.ShapeDtypeStruct((3, depth + FEAT, width), bf16),
        compiler_params=pltpu.CompilerParams(vmem_limit_bytes=VMEM_LIMIT),
        cost_estimate=pl.CostEstimate(
            flops=6 * rows * depth * width, bytes_accessed=8 * rows * depth, transcendentals=0
        ),
        name="weigh_input",
    )(hidden, *[item for part in parts for item in part])


def unpack_kernel(in_ref, *out_refs):
    at = 0
    for out_ref in out_refs:
        rows = out_ref.shape[0]
        out_ref[...] = in_ref[0, at:at + rows].astype(f32)
        at += rows


def unpack(shares, parts):
    count, total, depth = shares.shape
    return pl.pallas_call(
        unpack_kernel,
        grid=(count,),
        in_specs=[pl.BlockSpec((1, total, depth), lambda i: (i, 0, 0))],
        out_specs=[pl.BlockSpec((rows, depth), lambda i: (i, 0)) for rows in parts],
        out_shape=[jax.ShapeDtypeStruct((count * rows, depth), f32) for rows in parts],
        compiler_params=params("arbitrary"),
        name="unpack",
    )(shares)


def weigh_plain(s, n_dp, first_low, act, ug, lg, context, ag, vec):
    depth = first_low.shape[1]
    parts = [nn(context, ag), tn(first_low, ug[s]), tn(act[s], lg)]
    parts = [item.astype(bf16).reshape(n_dp, -1, depth) for item in parts]
    parts.append(jnp.broadcast_to(vec[s][None], (n_dp, FEAT, depth)))
    return jnp.concatenate(parts, axis=1)


def cross(value, count, bits):
    return lax.ppermute(value, "mp", [(i, i ^ bits) for i in range(count)])


def tie(values, others):
    return lax.optimization_barrier((values, others))[0]


def trade(value):
    return lax.all_to_all(value, "mp", 0, 0, tiled=True)


def swap(value, count, bit):
    return lax.ppermute(value, "dp", [(i, i ^ bit) for i in range(count)])


def hop(came, k, count):
    ahead, behind = came
    return (
        lax.ppermute(ahead, "mp", [(i, i + 1) for i in range(k - 1, count - 1)]),
        lax.ppermute(behind, "mp", [(i, i - 1) for i in range(1, count - k + 1)]),
    )


def finish_line(value, hops, me, count):
    while len(hops) < count - 1:
        hops = hops + [hop(hops[-1] if hops else (value, value), len(hops) + 1, count)]
    total = join_line(me, value, *zip(*hops))
    return total.reshape((-1,) + value.shape[1:])


def local(
    n_dp,
    n_mp,
    hidden,
    lengths,
    query_weight,
    query_bias,
    key_weight,
    key_bias,
    value_weight,
    value_bias,
    out_weight,
    out_bias,
    first_gain,
    first_shift,
    up_weight,
    up_bias,
    down_weight,
    down_bias,
    second_gain,
    second_shift,
    out_grad,
):
    rows, depth = hidden.shape
    width = query_weight.shape[1]
    hidden_local = up_weight.shape[1]
    heads = width // HEAD
    own = rows // n_mp
    me = lax.axis_index("mp")
    peer = lax.axis_index("dp")
    steps = range(n_mp)
    place = jnp.stack([me, peer]).astype(jnp.int32)

    def share_of(weight):
        share = weight.shape[0] // n_dp
        return lax.dynamic_slice_in_dim(weight, peer * share, share, 0)

    def gather_plane(value):
        return lax.all_gather(value, "dp", axis=0)

    def gather_others(weight):
        shares = [gather_plane(cross(share_of(weight), n_mp, s)) for s in steps if s]
        return jnp.stack([item.reshape(weight.shape) for item in shares])

    weights = [out_weight, up_weight, down_weight]
    qt, kt, kn, vt, vn, cosine, sine, turned = project(
        lengths, hidden, query_weight, key_weight, value_weight, query_bias, key_bias, value_bias
    )
    chips = n_dp // 2
    packed = n_dp if width // n_dp % FEAT == 0 and hidden_local == depth else 0
    splits = [1, n_mp - 1, n_mp] if n_mp > 2 else [1, n_mp]
    if packed:
        half = hidden_local // 2
        up_rows, down_rows, out_rows = depth // chips, half // chips, width // n_dp
        pack = make_pack(place, chips, up_weight, down_weight, out_weight, up_bias)
        marks = [up_rows, up_rows + 2 * (down_rows + out_rows)]
        crossed = {0: pack}
        for s in steps:
            if s & (s - 1) == 0 and s:
                crossed[s] = cross(pack, n_mp, s)
        bits = [2 << b for b in range(chips.bit_length() - 1)]

        def begin(group):
            group = jnp.stack([crossed[s] for s in group])[None]
            return [group[:, :, :marks[0]], group[:, :, marks[0]:marks[1]]]

        def double(held, step):
            came = [swap(held[0], n_dp, bits[step]), swap(held[1], n_dp, bits[-1 - step])]
            return came, lambda came: [jnp.concatenate(pair) for pair in zip(held, came)]

    contexts, tops, results = [None] * n_mp, [None] * n_mp, []

    def attend_next(after, count=1):
        first = n_mp - 1 - len(results)
        ctx, top = attend(place, first, count, n_mp, qt, kn, vt, after)
        for i in range(count):
            s = first - i
            tops[s] = top[i]
            results.append(ctx)
            contexts[s] = cross(ctx[i], n_mp, s) if s else ctx[i]

    if packed and n_mp == 4 and len(bits) == 2:
        attend_next([])
        crossed[1], crossed[2] = tie((crossed[1], crossed[2]), results[0])
        crossed[3] = cross(crossed[2], n_mp, 1)
        near = begin([1, 2])
        near_came, near_join = double(near, 0)
        attend_next([])
        near_came, crossed[3], contexts[3] = tie(
            (near_came, crossed[3], contexts[3]), results[1]
        )
        near = near_join(near_came)
        near_came, near_join = double(near, 1)
        far = begin([3])
        far_came, far_join = double(far, 0)
        attend_next([contexts[3]] + near + far, 2)
        near_came, far_came, contexts[2] = tie(
            (near_came, far_came, contexts[2]), results[3]
        )
        near, far = near_join(near_came), far_join(far_came)
        far_came, far_join = double(far, 1)
        near_other = [swap(item, n_dp, 1) for item in near]
        far = tie(far_join(far_came), contexts[1])
        banks = near + near_other + far + [swap(item, n_dp, 1) for item in far]
    else:
        for s in steps:
            attend_next([])
        if packed:
            banks = []
            for s in steps:
                if s & (s - 1):
                    crossed[s] = cross(crossed[s & (s - 1)], n_mp, s & -s)
            for i in range(len(splits) - 1):
                held = begin(range(splits[i], splits[i + 1]))
                for step in range(len(bits)):
                    came, join = double(held, step)
                    held = join(came)
                banks += held + [swap(item, n_dp, 1) for item in held]
    if packed:
        biases = [crossed[s][marks[1]:marks[1] + FEAT] for s in steps]
        biases = jnp.stack(
            [
                jnp.concatenate([jnp.sum(item[3 * c:3 * c + 3].astype(f32), 0) for c in range(2)])
                for item in biases
            ]
        )
    else:
        banks = [gather_others(item) for item in weights]
        biases = jnp.stack([up_bias] + [cross(up_bias, n_mp, s) for s in steps if s])
    tops = jnp.stack(tops)

    vectors = jnp.stack(
        [out_bias, first_gain, first_shift, down_bias, second_gain, second_shift]
    )
    result_own, first_low, act, slope, lg, normed, inv, second_back, some = feed(
        place, n_mp, packed, splits, hidden, out_grad, contexts, weights, banks, biases, vectors,
    )
    if packed:
        share = share_of(turned)
        shares = tie([cross(share, n_mp, s) for s in steps if s], lg)
        input_bank = gather_plane(jnp.stack(shares))
    else:
        input_bank = gather_others(turned)
    ug, ag, first_back, dctx, vec = feed_back(
        place, n_mp, packed, splits, contexts, weights, banks, slope, lg, normed, inv,
        second_back, some, first_gain[None],
    )
    came = tie(hop((result_own, result_own), 1, n_mp), lg if n_mp == 2 else ag)
    hops = [came]
    grads = trade(dctx)

    if packed:
        stacked = jnp.stack([item[:width] for item in contexts])
        operands = (first_low, act, ug, lg, stacked, ag, vec)
        half = n_mp // 2
        pieces = weigh(n_dp, width, 0, half, *operands, None, list(came))
        pieces = weigh(n_dp, width, half, n_mp - half, *operands, pieces, [grads])
        ready = [pieces]
        pieces = lax.psum_scatter(
            tie(pieces, input_bank), "dp", scatter_dimension=0, tiled=False
        )
        odd, even = pieces[1::2], pieces[::2]
    else:
        parts, ready = [], []
        for s in steps:
            part = weigh_plain(s, n_dp, first_low, act, ug, lg, contexts[s], ag, vec)
            parts.append(lax.psum_scatter(part, "dp", scatter_dimension=0, tiled=False))
        odd, even = jnp.stack(parts[1::2]), jnp.stack(parts[::2])

    parts, received = [], []
    for h in range(heads):
        after = ready if h == 0 else [came]
        after = jax.tree.leaves(after + [hops[0]]) if h == 0 else jax.tree.leaves(after)
        if h > 1:
            after.append(received[h - 2])
        *part, send = attend_back(
            place, h, n_mp, qt, kt, kn, vn, grads, tops, cosine, sine, after
        )
        if len(hops) < n_mp - 1:
            came = tie(hop(hops[-1], len(hops) + 1, n_mp), part[0])
            hops.append(came)
        else:
            came = []
        parts.append(part)
        received.append(trade(tie(send, received[-1]) if h else send))
    result = finish_line(result_own, hops, place, n_mp)
    last = heads - 1
    sums_in = weigh_input(hidden, tie(parts, received[max(last - 1, 0)]))
    input_grad = input_gradient(
        place, n_mp, packed, 0, tie(first_back, sums_in), turned, input_bank, received[:last], f32
    )
    odd = tie(cross(tie(odd, sums_in), n_mp, 1), input_grad)
    hidden_own = input_gradient(
        place, n_mp, packed, last, input_grad, turned, input_bank, received[last:], bf16
    )
    first_hop = hop((hidden_own, hidden_own), 1, n_mp)
    odd = tie(odd, hidden_own)
    input_sums = lax.psum(sums_in, "dp")
    tail = [first_hop]
    if n_mp > 2:
        tail.append(tie(hop(first_hop, 2, n_mp), input_sums))
    hidden_grad = finish_line(hidden_own, tail, place, n_mp)
    totals = [even[i].astype(f32) + odd[i].astype(f32) for i in range(n_mp // 2)]
    bit = 2
    while len(totals) > 1:
        sent = jnp.stack(totals[1::2]).astype(bf16)
        other = cross(sent, n_mp, bit)
        totals = [item + other[i].astype(f32) for i, item in enumerate(totals[::2])]
        bit *= 2
    total = totals[0]
    matrices = gather_plane(tie(total[:-FEAT].astype(bf16), first_hop))
    if packed:
        out_weight_grad, up_weight_grad, down_weight_grad = unpack(
            matrices, (width // n_dp, depth // n_dp, hidden_local // n_dp)
        )
    else:
        marks = [0, width, width + hidden_local, width + 2 * hidden_local]
        shapes = [(width, depth), (depth, hidden_local), (hidden_local, depth)]
        out_weight_grad, up_weight_grad, down_weight_grad = (
            matrices[:, marks[i] // n_dp:marks[i + 1] // n_dp].reshape(shapes[i]).astype(f32)
            for i in range(3)
        )
    sums = total[-FEAT:]
    input_sums = input_sums.astype(f32)
    input_grads = []
    for item in input_sums:
        input_grads += [item[:depth], item[depth]]
    return (
        result,
        hidden_grad,
        *input_grads,
        out_weight_grad,
        sums[1],
        sums[2],
        sums[3],
        up_weight_grad,
        sums[0, :hidden_local],
        down_weight_grad,
        sums[4],
        sums[5],
        sums[6],
    )


def solution(mesh):
    in_specs = (
        P("dp", None),
        P("dp", None),
        P(None, "mp"),
        P("mp"),
        P(None, "mp"),
        P("mp"),
        P(None, "mp"),
        P("mp"),
        P("mp", None),
        P(),
        P(),
        P(),
        P(None, "mp"),
        P("mp"),
        P("mp", None),
        P(),
        P(),
        P(),
        P("dp", None),
    )
    out_specs = (
        P("dp", None),
        P("dp", None),
        P(None, "mp"),
        P("mp"),
        P(None, "mp"),
        P("mp"),
        P(None, "mp"),
        P("mp"),
        P("mp", None),
        P(),
        P(),
        P(),
        P(None, "mp"),
        P("mp"),
        P("mp", None),
        P(),
        P(),
        P(),
    )
    body = functools.partial(local, mesh.shape["dp"], mesh.shape["mp"])
    return jax.shard_map(
        body, mesh=mesh, in_specs=in_specs, out_specs=out_specs, check_vma=False
    )
```
